512 devices in a mesh: blk: 32 (over y, x), lev: 16 (over z, core).
Axes of the slice: x: 4, y: 8, z: 8, core: 2. Of those that a mesh axis runs over, the one named last changes fastest.
Arguments:
- grid_values: float32 [64, 2, 64, 6144], P('blk', None, 'lev'), may hold values from -6 to 6
- quad_weight: float32 [64], P('blk'), may hold values from 0.3 to 3
- legendre: bfloat16 [1024, 2, 64, 512], P('blk'), may hold values from -0.75 to 0.75
- vertical_modes: float32 [64, 64], replicated, may hold values from -0.75 to 0.75
- eigenvalues: float32 [64], replicated, may hold values from 0.05 to 5
- pair_latitude: int32 [64], P('blk'), may hold values from 0 to 1279, as said below
- wave_slot: int32 [1024], replicated, may hold values from 0 to 1023, each once
Outputs:
- new_grid: float32 [64, 2, 64, 6144], P('blk', None, 'lev')
The draws below stay inside these ranges and needn't reach their ends.
Inputs may be any that keep to these rules, and one draw needn't show every extreme that they name: `pair_latitude`: distinct northern cycle indices; cycle r has 20 + 4 r points and so has its southern mirror; cycles 0 and 1279 are always among them. `wave_slot`: each wavenumber is held at exactly one position.
All inputs are finite; a program needn't handle non-finite values.
Results may differ from the reference program's by a relative error of at most 0.0043.
Values may be sent and summed in bfloat16 or wider, within the bound.
A program may use at most 64 MiB of HBM per device.

```python
import math
import jax
import jax.numpy as jnp
from jax import lax

NORTH_CYCLES = 1280
WAVES = 1024
PAIRS = 64
LEVELS = 64
HALF = 512
PSLOT = 6144


def draw_pair_latitude(key, part):
    key = jax.random.fold_in(key, 11)
    first_key, second_key = jax.random.split(key)
    middle = jax.random.permutation(first_key, NORTH_CYCLES - 2)[:PAIRS - 2].astype(jnp.int32) + 1
    ends = jnp.array([0, NORTH_CYCLES - 1], dtype=jnp.int32)
    chosen = jnp.concatenate([ends, middle])
    return jax.random.permutation(second_key, chosen).astype(jnp.int32)


def level_of(rng, dims, cuts, least, largest):
    gain = 1.0
    for dim, shards_of in cuts:
        heights = jax.random.uniform(jax.random.fold_in(jax.random.fold_in(rng, 6), dim), (shards_of,), jnp.float32, least / len(cuts), largest / len(cuts))
        gain = gain * jnp.repeat(jnp.exp(heights), dims[dim] // shards_of).reshape((-1,) + (1,) * (len(dims) - 1 - dim))
    return gain


def scatter_about(rng, dims, width, bound, cuts=(), kind=jnp.bfloat16):
    drawn = width * jax.random.normal(rng, dims, jnp.float32)
    if cuts:
        drawn = drawn * level_of(rng, dims, cuts, -0.22, 0.18)
    return jnp.clip(drawn, -bound, bound).astype(kind)


def setup_inputs(seed: int = 0) -> dict:
    streams_of = jax.random.split(jax.random.key(seed), 8)
    return {
        "grid_values": scatter_about(streams_of[0], (PAIRS, 2, LEVELS, PSLOT), 1.0, 6.0, ((0, 32), (2, 16)), jnp.float32),
        "quad_weight": jnp.clip(jnp.exp(math.log(3.0) - 2.3025851 * jax.random.uniform(streams_of[1], (PAIRS,), jnp.float32) ** level_of(streams_of[1], (PAIRS,), ((0, 32),), -0.2, 0.2)), 0.3, 3.0),
        "legendre": scatter_about(streams_of[2], (WAVES, 2, PAIRS, HALF), PAIRS ** -0.5, 0.75, ((0, 32),)),
        "vertical_modes": scatter_about(streams_of[3], (LEVELS, LEVELS), LEVELS ** -0.5, 0.75, (), jnp.float32),
        "eigenvalues": jnp.clip(jnp.exp(jax.random.uniform(streams_of[4], (LEVELS,), jnp.float32, math.log(0.05), math.log(5.0))), 0.05, 5.0),
        "pair_latitude": draw_pair_latitude(jax.random.fold_in(streams_of[7], 71), 0),
        "wave_slot": jax.random.permutation(streams_of[6], WAVES).astype(jnp.int32),
    }


TWO_PI = 6.283185307179586
IMPLICIT_FACTOR = 4.0


def point_table(points):
    offsets = jnp.arange(128, dtype=jnp.int32)
    wave_index = jnp.arange(WAVES, dtype=jnp.int32)
    phases = (offsets[None, :, None] * wave_index[None, None, :]) % points[:, None, None]
    angles = TWO_PI * phases.astype(jnp.float32) / points[:, None, None].astype(jnp.float32)
    return jnp.concatenate([jnp.cos(angles), -jnp.sin(angles)], axis=2)


def block_turns(points, first_block):
    block_index = (first_block + jnp.arange(8, dtype=jnp.int32)).astype(jnp.int32)
    wave_index = jnp.arange(WAVES, dtype=jnp.int32)
    phases = (wave_index[None, None, :] * (128 * block_index)[None, :, None]) % points[:, None, None]
    angles = TWO_PI * phases.astype(jnp.float32) / points[:, None, None].astype(jnp.float32)
    return jnp.cos(angles), jnp.sin(angles)


def analyse(row_field, points, block_count):
    line_count, level_count, slot_count = row_field.shape
    point_index = jnp.arange(slot_count, dtype=jnp.int32)
    live_mask = (point_index[None, :] < points[:, None]).astype(jnp.float32)
    grouped = (row_field * live_mask[:, None, :]).reshape(line_count, level_count, slot_count // 1024, 8, 128)
    dft_table = point_table(points)

    def group_step(group, sums):
        real_sum, imag_sum = sums
        point_piece = lax.dynamic_index_in_dim(grouped, group, 2, keepdims=False)
        inner_sum = jnp.einsum('rlut,rtf->rluf', point_piece, dft_table, precision=lax.Precision.HIGHEST)
        cosine, sine_part = block_turns(points, 8 * group)
        cos_wide = cosine[:, None]
        sin_wide = sine_part[:, None]
        cos_sum = inner_sum[..., :WAVES]
        sin_sum = inner_sum[..., WAVES:]
        real_sum = real_sum + jnp.sum(cos_wide * cos_sum + sin_wide * sin_sum, axis=2)
        imag_sum = imag_sum + jnp.sum(cos_wide * sin_sum - sin_wide * cos_sum, axis=2)
        return real_sum, imag_sum

    zeros = jnp.zeros((line_count, level_count, WAVES), jnp.float32)
    real_sum, imag_sum = lax.fori_loop(0, block_count, group_step, (zeros, zeros))
    wave_index = jnp.arange(WAVES, dtype=jnp.int32)
    kept = (2 * wave_index[None, :] < points[:, None]).astype(jnp.float32) / points[:, None].astype(jnp.float32)
    return real_sum * kept[:, None], imag_sum * kept[:, None]


def synthesise(real_part, imag_part, points, block_count, slot_count):
    line_count, level_count, wave_total = real_part.shape
    dft_table = point_table(points)
    wave_index = jnp.arange(WAVES, dtype=jnp.int32)
    kept = (2 * wave_index[None, :] < points[:, None]).astype(jnp.float32)
    doubling = jnp.where(wave_index == 0, 1.0, 2.0).astype(jnp.float32)
    real_part = real_part * (kept * doubling[None, :])[:, None]
    imag_part = imag_part * (kept * doubling[None, :])[:, None]

    def group_step(group, output):
        cosine, sine_part = block_turns(points, 8 * group)
        cos_wide = cosine[:, None]
        sin_wide = sine_part[:, None]
        turned_real = cos_wide * real_part[:, :, None] - sin_wide * imag_part[:, :, None]
        turned_imag = sin_wide * real_part[:, :, None] + cos_wide * imag_part[:, :, None]
        joined = jnp.concatenate([turned_real, turned_imag], axis=3)
        values = jnp.einsum('rluf,rtf->rlut', joined, dft_table, precision=lax.Precision.HIGHEST)
        values = values.reshape(line_count, level_count, 1024)
        return lax.dynamic_update_slice_in_dim(output, values, 1024 * group, 2)

    output = lax.fori_loop(0, block_count, group_step, jnp.zeros((line_count, level_count, slot_count), jnp.float32))
    point_index = jnp.arange(slot_count, dtype=jnp.int32)
    live_mask = (point_index[None, :] < points[:, None]).astype(jnp.float32)
    return output * live_mask[:, None, :]


def degrees(slot_waves, first_row, row_count):
    rows = first_row + jnp.arange(row_count, dtype=jnp.int32)
    parity = jnp.arange(2, dtype=jnp.int32)
    return slot_waves[:, None, None] + parity[None, :, None] + 2 * rows[None, None, :]


def vertical_solve(spectral, degree, vertical_modes, eigenvalues):
    degree_real = degree.astype(jnp.float32)
    degree_term = degree_real * (degree_real + 1.0) * (IMPLICIT_FACTOR / (WAVES * (WAVES - 1)))
    stiffness = degree_term[..., None] * eigenvalues
    damping = stiffness / (1.0 + stiffness)
    modal_part = jnp.einsum('...lc,lj->...jc', spectral, vertical_modes, precision=lax.Precision.HIGHEST)
    modal_part = modal_part * damping[..., None]
    return spectral - jnp.einsum('...jc,lj->...lc', modal_part, vertical_modes, precision=lax.Precision.HIGHEST)


def reference(grid_values, quad_weight, legendre, vertical_modes, eigenvalues, pair_latitude, wave_slot):
    points = 20 + 4 * jnp.repeat(pair_latitude, 2)
    row_field = grid_values.reshape(PAIRS * 2, LEVELS, PSLOT)
    block_count = PSLOT // 1024

    def forward_row(packed):
        one_field, one_points = packed
        real_part, imag_part = analyse(one_field[None], one_points[None], block_count)
        return real_part[0], imag_part[0]

    real_part, imag_part = lax.map(forward_row, (row_field, points))
    fourier = jnp.stack([real_part, imag_part], axis=2).reshape(PAIRS, 2, LEVELS, 2, WAVES)
    northern = fourier[:, 0]
    southern = fourier[:, 1]
    weight = quad_weight[:, None, None, None]
    folded = jnp.stack([weight * (northern + southern), weight * (northern - southern)], axis=1).astype(jnp.bfloat16)
    by_slot = jnp.moveaxis(jnp.take(folded, wave_slot, axis=4), 4, 0)

    def per_slot(packed):
        slot_table, slot_data, slot_wave = packed
        table_wide = slot_table.astype(jnp.float32)
        spectral = jnp.einsum('qph,pqlc->qhlc', table_wide, slot_data.astype(jnp.float32))
        degree = degrees(slot_wave[None], 0, HALF)[0]
        spectral = spectral * (degree <= WAVES - 1).astype(jnp.float32)[:, :, None, None]
        solved = vertical_solve(spectral, degree, vertical_modes, eigenvalues).astype(jnp.bfloat16)
        return jnp.einsum('qph,qhlc->pqlc', table_wide, solved.astype(jnp.float32)).astype(jnp.bfloat16)

    synthesized = lax.map(per_slot, (legendre, by_slot, wave_slot))
    placed_back = jnp.moveaxis(synthesized, 0, 4)
    slot_of = jnp.zeros(WAVES, jnp.int32).at[wave_slot].set(jnp.arange(WAVES, dtype=jnp.int32))
    natural_order = jnp.take(placed_back, slot_of, axis=4).astype(jnp.float32)
    symmetric = natural_order[:, 0]
    antisymmetric = natural_order[:, 1]
    hemispheres = jnp.stack([symmetric + antisymmetric, symmetric - antisymmetric], axis=1)
    hemispheres = hemispheres.reshape(PAIRS * 2, LEVELS, 2, WAVES)

    def backward_row(packed):
        one_real, one_imag, one_points = packed
        return synthesise(one_real[None], one_imag[None], one_points[None], block_count, PSLOT)[0]

    output = lax.map(backward_row, (hemispheres[:, :, 0], hemispheres[:, :, 1], points))
    return output.reshape(PAIRS, 2, LEVELS, PSLOT)
```

```python
import jax
import jax.numpy as jnp
from jax import lax
from jax.experimental import pallas as pl
from jax.experimental.pallas import tpu as pltpu
from jax.sharding import PartitionSpec as P

MESH = pl.DeviceIdType.MESH
BF16 = jnp.bfloat16
F32 = jnp.float32

WAVES = 1024
HALF = 512
LEVELS = 64
NB = 32
NL = 16
SPAN = 256
BLOCKS = 22
ROWS = 8 * BLOCKS
TILES = WAVES // 128
LIVE = BLOCKS * SPAN
PSLOT = 6144
IMPLICIT_FACTOR = 4.0
PI = 3.141592653589793


def iota(shape, dim):
    return lax.broadcasted_iota(jnp.int32, shape, dim)


def dot(a, b):
    return jnp.dot(a, b, preferred_element_type=F32)


def dot_nt(a, b):
    return lax.dot_general(a, b, (((1,), (1,)), ((), ())), preferred_element_type=F32)


def dot_tn(a, b):
    return lax.dot_general(a, b, (((0,), (0,)), ((), ())), preferred_element_type=F32)


def split(x):
    high = x.astype(BF16)
    return high, (x - high.astype(F32)).astype(BF16)


def rotation(phase, points, inverse):
    turns = jnp.floor(phase * inverse + 0.5)
    x = (phase - turns * points) * inverse
    z = x * x
    sine = 0.0
    cosine = 0.0
    sin_terms = [PI]
    cos_terms = [1.0]
    for k in range(1, 7):
        sin_terms.append(-sin_terms[-1] * PI * PI / ((2 * k) * (2 * k + 1)))
        cos_terms.append(-cos_terms[-1] * PI * PI / ((2 * k - 1) * (2 * k)))
    sine = jnp.full_like(z, sin_terms[6])
    cosine = jnp.full_like(z, cos_terms[6])
    for k in range(5, -1, -1):
        sine = sine * z + sin_terms[k]
        cosine = cosine * z + cos_terms[k]
    sine = sine * x
    return 1.0 - 2.0 * sine * sine, -2.0 * sine * cosine


def turn(a, b):
    return a[0] * b[0] - a[1] * b[1], a[0] * b[1] + a[1] * b[0]


def stack(parts):
    return jnp.concatenate(parts, axis=0)


def kernel(
    grid_hbm, weight_ref, legendre_hbm, modes_ref, rates_ref, cycle_ref, slot_ref, slot_smem,
    out_ref,
    grid_ref, raw_ref, wave_ref, x_ref, table_ref, turn_ref, four_ref,
    s1_ref, r1_ref, s2_ref, r2_ref, s3_ref, r3_ref, s4_ref, r4_ref,
    leg_ref, mode1_ref, mode2_ref, damp_ref, solved_ref, turned_ref,
    load_sem, send_sem, recv_sem,
):
    blk = lax.axis_index("blk")
    lev = lax.axis_index("lev")

    barrier = pltpu.get_barrier_semaphore()

    def greet_blk(k, carry):
        pl.semaphore_signal(barrier, inc=1, device_id=((blk + k) % NB, lev), device_id_type=MESH)
        return carry

    def greet_lev(k, carry):
        pl.semaphore_signal(barrier, inc=1, device_id=(blk, (lev + k) % NL), device_id_type=MESH)
        return carry

    grid_copy = pltpu.make_async_copy(grid_hbm, grid_ref, load_sem.at[0])
    grid_copy.start()
    legendre_copy = pltpu.make_async_copy(
        legendre_hbm.at[pl.ds(2 * lev, 2)], raw_ref, load_sem.at[1]
    )
    legendre_copy.start()
    lax.fori_loop(1, NB, greet_blk, 0)
    lax.fori_loop(1, NL, greet_lev, 0)

    column = iota((128, WAVES), 1)
    pick = (iota((128, WAVES), 0) == 32 * (column & 3) + (column >> 5)).astype(F32).astype(BF16)
    slots = slot_ref[...]
    halves = stack([slots >> 5, slots & 31]).astype(F32).astype(BF16)
    spread = dot(halves, pick)
    column = iota((8, WAVES), 1)
    mine = iota((8, WAVES), 0) == ((column & 31) >> 2)
    spread = jnp.where(mine, 32.0 * spread[:8] + spread[8:], 0.0)
    waves = jnp.sum(spread, axis=0, keepdims=True)
    for tile in range(TILES):
        wave_ref[tile] = jnp.broadcast_to(waves[:, 128 * tile : 128 * (tile + 1)], (8, 128))

    def points_of(i):
        return 20 + 4 * cycle_ref[i]

    grid_copy.wait()

    def fold_step(step, carry):
        i = step // (BLOCKS // 2)
        k = step % (BLOCKS // 2)
        points = points_of(i)
        scale = jnp.full((4, SPAN), weight_ref[i], F32) / jnp.full((4, SPAN), points, jnp.int32).astype(F32)
        rows = []
        for half in range(2):
            start = pl.multiple_of(512 * k + 256 * half, 256)
            live = iota((4, SPAN), 1) + start < points
            north = grid_ref[i, 0, :, pl.ds(start, SPAN)]
            south = grid_ref[i, 1, :, pl.ds(start, SPAN)]
            rows.append(jnp.where(live, (north + south) * scale, 0.0))
            rows.append(jnp.where(live, (north - south) * scale, 0.0))
        high, low = split(stack(rows))
        x_ref[i, 0, pl.ds(pl.multiple_of(16 * k, 16), 16), :] = high
        x_ref[i, 1, pl.ds(pl.multiple_of(16 * k, 16), 16), :] = low
        return carry

    lax.fori_loop(0, BLOCKS, fold_step, 0)

    def analyse_step(step, carry):
        i = step // TILES
        tile = step % TILES
        points = jnp.full((8, 128), points_of(i), jnp.int32).astype(F32)
        inverse = 1.0 / points
        wave = wave_ref[tile]
        row = iota((8, 128), 0)
        place = row.astype(F32)
        extra = jnp.where(row == 0, 8.0, jnp.where(row == 1, 128.0, 2048.0))
        fine = rotation(place * wave, points, inverse)
        coarse = rotation(16.0 * place * wave, points, inverse)
        block = rotation(256.0 * place * wave, points, inverse)
        jump = rotation(extra * wave, points, inverse)

        def spread_row(pair, k, rows=8):
            return tuple(jnp.broadcast_to(part[k : k + 1], (rows, 128)) for part in pair)

        fine_next = turn(fine, spread_row(jump, 0))
        coarse_next = turn(coarse, spread_row(jump, 1))
        leap = spread_row(jump, 2)
        kept = (2.0 * wave < points).astype(F32)
        block = (block[0] * kept, block[1] * kept)
        block_1 = turn(block, leap)
        block_2 = turn(block_1, leap)

        high = [[], []]
        low = [[], []]
        for a in range(16):
            lead = spread_row(coarse if a < 8 else coarse_next, a % 8)
            first = turn(lead, fine)
            second = turn(lead, fine_next)
            for part in range(2):
                h, l = split(stack([first[part], second[part]]))
                high[part].append(h)
                low[part].append(l)
        for part in range(2):
            table_ref[i, tile, :, 128 * part : 128 * (part + 1)] = stack(high[part])
        fine_table = table_ref[i, tile]
        rest_table = jnp.concatenate([stack(low[0]), stack(low[1])], axis=1)
        x_high = x_ref[i, 0]
        sums = dot(x_high, fine_table) + dot(x_ref[i, 1], fine_table) + dot(x_high, rest_table)
        real = jnp.zeros((8, 128), F32)
        imag = jnp.zeros((8, 128), F32)
        for u in range(BLOCKS):
            c, s = spread_row((block, block_1, block_2)[u // 8], u % 8)
            turn_ref[i, tile, 0, u] = c
            turn_ref[i, tile, 1, u] = s
            p, q = sums[8 * u : 8 * u + 8, :128], sums[8 * u : 8 * u + 8, 128:]
            real = real + (c * p - s * q)
            imag = imag + (c * q + s * p)
        start = pl.multiple_of(16 * tile, 16)
        four_ref[i, pl.ds(start, 8), :] = real
        four_ref[i, pl.ds(start + 8, 8), :] = imag
        return carry

    lax.fori_loop(0, 2 * TILES, analyse_step, 0)

    for i in range(2):
        flipped = four_ref[i].T
        for a in range(4):
            s1_ref[pl.ds(2 * a + i, NB, stride=8), :] = flipped[NB * a : NB * (a + 1)]
    own = pl.ds(pl.multiple_of(8 * blk, 8), 8)
    r1_ref[own, :] = s1_ref[own, :]
    pl.semaphore_wait(barrier, NB + NL - 2)

    def send_blk(source, target, sem):
        def step(k, carry):
            other = (blk + k) % NB
            pltpu.make_async_remote_copy(
                src_ref=source.at[pl.ds(pl.multiple_of(8 * other, 8), 8)],
                dst_ref=target.at[own],
                send_sem=send_sem.at[sem],
                recv_sem=recv_sem.at[sem],
                device_id=(other, lev),
                device_id_type=MESH,
            ).start()
            return carry

        lax.fori_loop(1, NB, step, 0)
        rows = pl.ds(0, 8 * (NB - 1))
        return pltpu.make_async_remote_copy(
            src_ref=source.at[rows], dst_ref=target.at[rows],
            send_sem=send_sem.at[sem], recv_sem=recv_sem.at[sem],
            device_id=((blk + 1) % NB, lev), device_id_type=MESH,
        )

    def send_lev(source, target, sem):
        def step(k, carry):
            other = (lev + k) % NL
            pltpu.make_async_remote_copy(
                src_ref=source.at[other],
                dst_ref=target.at[lev],
                send_sem=send_sem.at[sem],
                recv_sem=recv_sem.at[sem],
                device_id=(blk, other),
                device_id_type=MESH,
            ).start()
            return carry

        lax.fori_loop(1, NL, step, 0)
        rows = pl.ds(0, NL - 1)
        return pltpu.make_async_remote_copy(
            src_ref=source.at[rows], dst_ref=target.at[rows],
            send_sem=send_sem.at[sem], recv_sem=recv_sem.at[sem],
            device_id=(blk, (lev + 1) % NL), device_id_type=MESH,
        )

    sent_1 = send_blk(s1_ref, r1_ref, 0)

    legendre_copy.wait()
    wave_0 = slot_smem[32 * blk + 2 * lev]
    wave_1 = slot_smem[32 * blk + 2 * lev + 1]
    row = iota((256, 256), 0)
    source = ((row >> 6) & 1) * 128 + (row >> 7) * 64 + 2 * (row & 31) + ((row >> 5) & 1)
    reorder = (iota((256, 256), 1) == source).astype(F32).astype(BF16)
    ordered = dot(reorder, raw_ref[...].reshape(256, HALF))
    row = iota((256, HALF), 0)
    degree = jnp.where(((row >> 6) & 1) == 0, wave_0, wave_1) + (row >> 7) + 2 * iota((256, HALF), 1)
    leg_ref[...] = jnp.where(degree <= WAVES - 1, ordered, 0.0).astype(BF16)

    def spread_rows(shape, row_dim):
        row = iota(shape, row_dim)
        return iota(shape, 1 - row_dim) == 4 * (row >> 4) + (row & 3)

    tall = spread_rows((256, LEVELS), 0).astype(F32).astype(BF16)
    wide = spread_rows((LEVELS, 256), 1).astype(F32).astype(BF16)
    same = ((iota((256, 256), 0) >> 2) & 3) == ((iota((256, 256), 1) >> 2) & 3)
    for part, modes in enumerate(split(modes_ref[...])):
        full = dot(tall, dot(modes, wide).astype(BF16))
        mode2_ref[256 * part : 256 * (part + 1), :] = jnp.where(same, full, 0.0).astype(BF16)
        full = dot(tall, dot_tn(modes, wide).astype(BF16))
        mode1_ref[256 * part : 256 * (part + 1), :] = jnp.where(same, full, 0.0).astype(BF16)

    rate = jnp.sum(
        jnp.where(spread_rows((256, LEVELS), 0), jnp.broadcast_to(rates_ref[...], (256, LEVELS)), 0.0),
        axis=1, keepdims=True,
    )
    rate = jnp.broadcast_to(rate, (256, 128))

    def damp_step(step, carry):
        e = step // 4
        chunk = step % 4
        wave = jnp.where(e == 0, wave_0, wave_1)
        degree = wave + ((iota((256, 128), 0) >> 2) & 1) + 2 * (iota((256, 128), 1) + 128 * chunk)
        degree = degree.astype(F32)
        term = degree * (degree + 1.0) * (IMPLICIT_FACTOR / (WAVES * (WAVES - 1)))
        stiffness = term * rate
        damp_ref[e, chunk] = stiffness / (1.0 + stiffness)
        return carry

    lax.fori_loop(0, 8, damp_step, 0)

    sent_1.wait_recv()

    for a in range(2):
        block = stack([r1_ref[pl.ds(4 * a + j, NB, stride=8), :] for j in range(4)]).T.astype(BF16)
        for t in range(8):
            s2_ref[2 * t + a] = block[16 * t : 16 * (t + 1)]
    r2_ref[lev] = s2_ref[lev]
    sent_2 = send_lev(s2_ref, r2_ref, 1)
    sent_2.wait_recv()

    data = r2_ref[...].reshape(256, 128)
    parity = (iota((256, 128), 0) >> 2) & 1
    side = iota((256, 128), 1) >> 6

    def chosen(q, e):
        return ((parity == q) & (side == e)).astype(F32).astype(BF16)

    def solve_step(step, carry):
        for e in range(2):
            columns = pl.ds(pl.multiple_of(256 * step, 256), 256)
            left = jnp.concatenate([data * chosen(0, e), data * chosen(1, e)], axis=1)
            spectral = dot(left, leg_ref[:, columns])
            high, low = split(spectral)
            both = dot(mode1_ref[...], high)
            modal = both[:256] + both[256:] + dot(mode1_ref[:256], low)
            damping = jnp.concatenate([damp_ref[e, 2 * step], damp_ref[e, 2 * step + 1]], axis=1)
            high, low = split(modal * damping)
            both = dot(mode2_ref[...], high)
            change = both[:256] + both[256:] + dot(mode2_ref[:256], low)
            solved_ref[e, :, columns] = (spectral - change).astype(BF16)
        return carry

    lax.fori_loop(0, 2, solve_step, 0)

    picked = []
    for e in range(2):
        back = dot_nt(solved_ref[e], leg_ref[...])
        picked.append(jnp.where(parity == 0, back[:, :128], back[:, 128:]))
    s3_ref[...] = jnp.where(side == 0, picked[0], picked[1]).astype(BF16).reshape(NL, 16, 128)
    r3_ref[lev] = s3_ref[lev]
    sent_3 = send_lev(s3_ref, r3_ref, 2)
    sent_3.wait_recv()

    for a in range(2):
        block = stack([r3_ref[2 * t + a] for t in range(8)]).astype(F32).T
        for j in range(4):
            s4_ref[pl.ds(4 * a + j, NB, stride=8), :] = block[NB * j : NB * (j + 1)]
    r4_ref[own, :] = s4_ref[own, :]
    sent_4 = send_blk(s4_ref, r4_ref, 3)
    out_ref[:, :, :, pl.ds(LIVE, PSLOT - LIVE)] = jnp.zeros((2, 2, 4, PSLOT - LIVE), F32)
    sent_4.wait_recv()

    for i in range(2):
        four_ref[i] = stack([r4_ref[pl.ds(2 * a + i, NB, stride=8), :] for a in range(4)]).T

    def turn_step(step, carry):
        i = step // TILES
        tile = step % TILES
        wave = wave_ref[tile]
        double = jnp.where(wave == 0.0, 1.0, 2.0)
        start = pl.multiple_of(16 * tile, 16)
        real = four_ref[i, pl.ds(start, 8), :] * double
        imag = four_ref[i, pl.ds(start + 8, 8), :] * double
        for k in range(BLOCKS // 2):
            reals, imags = [], []
            for u in (2 * k, 2 * k + 1):
                c = turn_ref[i, tile, 0, u]
                s = turn_ref[i, tile, 1, u]
                reals.append(real * c + imag * s)
                imags.append(imag * c - real * s)
            for part, rows in enumerate((reals, imags)):
                high, low = split(stack(rows))
                lanes = slice(128 * part, 128 * (part + 1))
                turned_ref[i, tile, 16 * k : 16 * k + 16, lanes] = high
                turned_ref[i, tile, ROWS + 16 * k : ROWS + 16 * k + 16, lanes] = low
        return carry

    lax.fori_loop(0, 2 * TILES, turn_step, 0)

    for i in range(2):
        left = jnp.concatenate([turned_ref[i, tile] for tile in range(TILES)], axis=1)
        right = jnp.concatenate([table_ref[i, tile] for tile in range(TILES)], axis=1)
        both = dot_nt(left, right)
        points = points_of(i)
        for u in range(BLOCKS):
            value = both[8 * u : 8 * u + 8] + both[ROWS + 8 * u : ROWS + 8 * u + 8]
            live = iota((4, SPAN), 1) + SPAN * u < points
            out_ref[i, 0, :, SPAN * u : SPAN * (u + 1)] = jnp.where(live, value[:4] + value[4:], 0.0)
            out_ref[i, 1, :, SPAN * u : SPAN * (u + 1)] = jnp.where(live, value[:4] - value[4:], 0.0)

    for sent in (sent_1, sent_2, sent_3, sent_4):
        sent.wait_send()


def shards(grid_values, quad_weight, legendre, vertical_modes, eigenvalues, pair_latitude, wave_slot):
    vmem = pl.BlockSpec(memory_space=pltpu.VMEM)
    smem = pl.BlockSpec(memory_space=pltpu.SMEM)
    hbm = pl.BlockSpec(memory_space=pl.ANY)
    return pl.pallas_call(
        kernel,
        out_shape=jax.ShapeDtypeStruct(grid_values.shape, F32),
        in_specs=[hbm, smem, hbm, vmem, vmem, smem, vmem, smem],
        out_specs=vmem,
        scratch_shapes=[
            pltpu.VMEM((2, 2, 4, PSLOT), F32),
            pltpu.VMEM((2, 2, 64, HALF), BF16),
            pltpu.VMEM((TILES, 8, 128), F32),
            pltpu.VMEM((2, 2, ROWS, SPAN), BF16),
            pltpu.VMEM((2, TILES, SPAN, 256), BF16),
            pltpu.VMEM((2, TILES, 2, BLOCKS, 8, 128), F32),
            pltpu.VMEM((2, 128, 128), F32),
            pltpu.VMEM((8 * NB, 128), F32),
            pltpu.VMEM((8 * NB, 128), F32),
            pltpu.VMEM((NL, 16, 128), BF16),
            pltpu.VMEM((NL, 16, 128), BF16),
            pltpu.VMEM((NL, 16, 128), BF16),
            pltpu.VMEM((NL, 16, 128), BF16),
            pltpu.VMEM((8 * NB, 128), F32),
            pltpu.VMEM((8 * NB, 128), F32),
            pltpu.VMEM((256, HALF), BF16),
            pltpu.VMEM((512, 256), BF16),
            pltpu.VMEM((512, 256), BF16),
            pltpu.VMEM((2, 4, 256, 128), F32),
            pltpu.VMEM((2, 256, HALF), BF16),
            pltpu.VMEM((2, TILES, 2 * ROWS, 256), BF16),
            pltpu.SemaphoreType.DMA((2,)),
            pltpu.SemaphoreType.DMA((4,)),
            pltpu.SemaphoreType.DMA((4,)),
        ],
        compiler_params=pltpu.CompilerParams(
            collective_id=0, has_side_effects=True, vmem_limit_bytes=62 * 1024 * 1024
        ),
        cost_estimate=pl.CostEstimate(flops=4_000_000_000, bytes_accessed=1_500_000, transcendentals=0),
    )(
        grid_values, quad_weight, legendre, vertical_modes, eigenvalues.reshape(1, LEVELS),
        pair_latitude, wave_slot.reshape(8, 128), wave_slot,
    )


def solution(mesh):
    in_specs = (
        P("blk", None, "lev", None),
        P("blk"),
        P("blk", None, None, None),
        P(),
        P(),
        P("blk"),
        P(),
    )
    out_specs = P("blk", None, "lev", None)
    return jax.shard_map(shards, mesh=mesh, in_specs=in_specs, out_specs=out_specs, check_vma=False)
```

```python
import jax
import jax.numpy as jnp
from jax import lax
from jax.experimental import pallas as pl
from jax.experimental.pallas import tpu as pltpu
from jax.sharding import PartitionSpec as P

MESH = pl.DeviceIdType.MESH
BF16 = jnp.bfloat16
F32 = jnp.float32

WAVES = 1024
HALF = 512
LEVELS = 64
NB = 32
NL = 16
SPAN = 256
BLOCKS = 22
ROWS = 8 * BLOCKS
TILES = WAVES // 128
LIVE = BLOCKS * SPAN
PSLOT = 6144
IMPLICIT_FACTOR = 4.0
PI = 3.141592653589793


def ring(step, size):
    return min(step, size - step)


BLK_PEERS = sorted(
    [(y, x) for y in range(8) for x in range(4) if (y, x) != (0, 0)],
    key=lambda d: (-ring(d[0], 8) - ring(d[1], 4), d),
)
LEV_PEERS = sorted(
    [(z, c) for z in range(8) for c in range(2) if (z, c) != (0, 0)],
    key=lambda d: (-ring(d[0], 8) - 0.5 * d[1], d),
)


def blk_peer(blk, peer):
    return (blk // 4 + peer[0]) % 8 * 4 + (blk % 4 + peer[1]) % 4


def lev_peer(lev, peer):
    return (lev // 2 + peer[0]) % 8 * 2 + (lev % 2 + peer[1]) % 2


def iota(shape, dim):
    return lax.broadcasted_iota(jnp.int32, shape, dim)


def dot(a, b):
    return jnp.dot(a, b, preferred_element_type=F32)


def dot_nt(a, b):
    return lax.dot_general(a, b, (((1,), (1,)), ((), ())), preferred_element_type=F32)


def dot_tn(a, b):
    return lax.dot_general(a, b, (((0,), (0,)), ((), ())), preferred_element_type=F32)


def split(x):
    high = x.astype(BF16)
    return high, (x - high.astype(F32)).astype(BF16)


def rotation(phase, points, inverse):
    turns = jnp.floor(phase * inverse + 0.5)
    x = (phase - turns * points) * inverse
    z = x * x
    sine = 0.0
    cosine = 0.0
    sin_terms = [PI]
    cos_terms = [1.0]
    for k in range(1, 7):
        sin_terms.append(-sin_terms[-1] * PI * PI / ((2 * k) * (2 * k + 1)))
        cos_terms.append(-cos_terms[-1] * PI * PI / ((2 * k - 1) * (2 * k)))
    sine = jnp.full_like(z, sin_terms[6])
    cosine = jnp.full_like(z, cos_terms[6])
    for k in range(5, -1, -1):
        sine = sine * z + sin_terms[k]
        cosine = cosine * z + cos_terms[k]
    sine = sine * x
    return 1.0 - 2.0 * sine * sine, -2.0 * sine * cosine


def turn(a, b):
    return a[0] * b[0] - a[1] * b[1], a[0] * b[1] + a[1] * b[0]


def stack(parts):
    return jnp.concatenate(parts, axis=0)


def kernel(
    grid_hbm, weight_ref, legendre_hbm, modes_ref, rates_ref, cycle_ref, slot_ref, slot_smem,
    out_ref,
    grid_ref, raw_ref, wave_ref, x_ref, table_ref, turn_ref, four_ref,
    rows_ref, s1_ref, r1_ref, s2_ref, r2_ref, s3_ref, r3_ref, s4_ref, r4_ref,
    leg_ref, mode1_ref, mode2_ref, damp_ref, solved_ref, turned_ref,
    load_sem, send_sem, recv_sem,
):
    blk = lax.axis_index("blk")
    lev = lax.axis_index("lev")

    barrier = pltpu.get_barrier_semaphore()

    grid_copy = pltpu.make_async_copy(grid_hbm, grid_ref, load_sem.at[0])
    grid_copy.start()
    legendre_copy = pltpu.make_async_copy(
        legendre_hbm.at[pl.ds(2 * lev, 2)], raw_ref, load_sem.at[1]
    )
    legendre_copy.start()
    for peer in BLK_PEERS:
        pl.semaphore_signal(barrier, inc=1, device_id=(blk_peer(blk, peer), lev), device_id_type=MESH)
    for peer in LEV_PEERS:
        pl.semaphore_signal(barrier, inc=1, device_id=(blk, lev_peer(lev, peer)), device_id_type=MESH)

    column = iota((128, WAVES), 1)
    pick = (iota((128, WAVES), 0) == 32 * (column & 3) + (column >> 5)).astype(F32).astype(BF16)
    slots = slot_ref[...]
    halves = stack([slots >> 5, slots & 31]).astype(F32).astype(BF16)
    spread = dot(halves, pick)
    column = iota((8, WAVES), 1)
    mine = iota((8, WAVES), 0) == ((column & 31) >> 2)
    spread = jnp.where(mine, 32.0 * spread[:8] + spread[8:], 0.0)
    waves = jnp.sum(spread, axis=0, keepdims=True)
    for tile in range(TILES):
        wave_ref[tile] = jnp.broadcast_to(waves[:, 128 * tile : 128 * (tile + 1)], (8, 128))

    def points_of(i):
        return 20 + 4 * cycle_ref[i]

    grid_copy.wait()

    def fold_step(step, carry):
        i = step // (BLOCKS // 2)
        k = step % (BLOCKS // 2)
        points = points_of(i)
        scale = jnp.full((4, SPAN), weight_ref[i], F32) / jnp.full((4, SPAN), points, jnp.int32).astype(F32)
        rows = []
        for half in range(2):
            start = pl.multiple_of(512 * k + 256 * half, 256)
            live = iota((4, SPAN), 1) + start < points
            north = grid_ref[i, 0, :, pl.ds(start, SPAN)]
            south = grid_ref[i, 1, :, pl.ds(start, SPAN)]
            rows.append(jnp.where(live, (north + south) * scale, 0.0))
            rows.append(jnp.where(live, (north - south) * scale, 0.0))
        high, low = split(stack(rows))
        x_ref[i, 0, pl.ds(pl.multiple_of(16 * k, 16), 16), :] = high
        x_ref[i, 1, pl.ds(pl.multiple_of(16 * k, 16), 16), :] = low
        return carry

    lax.fori_loop(0, BLOCKS, fold_step, 0)

    def analyse_step(step, carry):
        i = step // TILES
        tile = step % TILES
        points = jnp.full((8, 128), points_of(i), jnp.int32).astype(F32)
        inverse = 1.0 / points
        wave = wave_ref[tile]
        row = iota((8, 128), 0)
        place = row.astype(F32)
        extra = jnp.where(row == 0, 8.0, jnp.where(row == 1, 128.0, 2048.0))
        fine = rotation(place * wave, points, inverse)
        coarse = rotation(16.0 * place * wave, points, inverse)
        block = rotation(256.0 * place * wave, points, inverse)
        jump = rotation(extra * wave, points, inverse)

        def spread_row(pair, k, rows=8):
            return tuple(jnp.broadcast_to(part[k : k + 1], (rows, 128)) for part in pair)

        fine_next = turn(fine, spread_row(jump, 0))
        coarse_next = turn(coarse, spread_row(jump, 1))
        leap = spread_row(jump, 2)
        kept = (2.0 * wave < points).astype(F32)
        block = (block[0] * kept, block[1] * kept)
        block_1 = turn(block, leap)
        block_2 = turn(block_1, leap)

        high = [[], []]
        low = [[], []]
        for a in range(16):
            lead = spread_row(coarse if a < 8 else coarse_next, a % 8)
            first = turn(lead, fine)
            second = turn(lead, fine_next)
            for part in range(2):
                h, l = split(stack([first[part], second[part]]))
                high[part].append(h)
                low[part].append(l)
        table = jnp.concatenate([stack(high[0]), stack(high[1])], axis=1)
        rest = jnp.concatenate([stack(low[0]), stack(low[1])], axis=1)
        table_ref[i, :, pl.ds(pl.multiple_of(256 * tile, 256), 256)] = table
        x_high = x_ref[i, 0]
        sums = dot(
            jnp.concatenate([x_high, x_ref[i, 1], x_high], axis=1),
            jnp.concatenate([table, table, rest], axis=0),
        )
        real = jnp.zeros((8, 128), F32)
        imag = jnp.zeros((8, 128), F32)
        for u in range(BLOCKS):
            c, s = spread_row((block, block_1, block_2)[u // 8], u % 8)
            turn_ref[i, tile, 0, u] = c
            turn_ref[i, tile, 1, u] = s
            p, q = sums[8 * u : 8 * u + 8, :128], sums[8 * u : 8 * u + 8, 128:]
            real = real + (c * p - s * q)
            imag = imag + (c * q + s * p)
        start = pl.multiple_of(16 * tile, 16)
        four_ref[i, pl.ds(start, 8), :] = real
        four_ref[i, pl.ds(start + 8, 8), :] = imag
        return carry

    lax.fori_loop(0, 2 * TILES, analyse_step, 0, unroll=4)

    for i in range(2):
        flipped = four_ref[i].T
        for a in range(4):
            rows_ref[pl.ds(2 * a + i, NB, stride=8), :] = flipped[NB * a : NB * (a + 1)]
    s1_ref[...] = rows_ref[...].astype(BF16).reshape(NB, 8, 128)
    r1_ref[blk] = s1_ref[blk]
    pl.semaphore_wait(barrier, NB + NL - 2)

    def send_blk(source, target, sem):
        for peer in BLK_PEERS:
            other = blk_peer(blk, peer)
            pltpu.make_async_remote_copy(
                src_ref=source.at[other],
                dst_ref=target.at[blk],
                send_sem=send_sem.at[sem],
                recv_sem=recv_sem.at[sem],
                device_id=(other, lev),
                device_id_type=MESH,
            ).start()
        rows = pl.ds(0, NB - 1)
        return pltpu.make_async_remote_copy(
            src_ref=source.at[rows], dst_ref=target.at[rows],
            send_sem=send_sem.at[sem], recv_sem=recv_sem.at[sem],
            device_id=(blk_peer(blk, BLK_PEERS[0]), lev), device_id_type=MESH,
        )

    def send_lev(source, target, sem):
        for peer in LEV_PEERS:
            other = lev_peer(lev, peer)
            pltpu.make_async_remote_copy(
                src_ref=source.at[other],
                dst_ref=target.at[lev],
                send_sem=send_sem.at[sem],
                recv_sem=recv_sem.at[sem],
                device_id=(blk, other),
                device_id_type=MESH,
            ).start()
        rows = pl.ds(0, NL - 1)
        return pltpu.make_async_remote_copy(
            src_ref=source.at[rows], dst_ref=target.at[rows],
            send_sem=send_sem.at[sem], recv_sem=recv_sem.at[sem],
            device_id=(blk, lev_peer(lev, LEV_PEERS[0])), device_id_type=MESH,
        )

    sent_1 = send_blk(s1_ref, r1_ref, 0)

    legendre_copy.wait()
    wave_0 = slot_smem[32 * blk + 2 * lev]
    wave_1 = slot_smem[32 * blk + 2 * lev + 1]
    row = iota((256, 256), 0)
    source = ((row >> 6) & 1) * 128 + (row >> 7) * 64 + 2 * (row & 31) + ((row >> 5) & 1)
    reorder = (iota((256, 256), 1) == source).astype(F32).astype(BF16)
    ordered = dot(reorder, raw_ref[...].reshape(256, HALF))
    row = iota((256, HALF), 0)
    degree = jnp.where(((row >> 6) & 1) == 0, wave_0, wave_1) + (row >> 7) + 2 * iota((256, HALF), 1)
    leg_ref[...] = jnp.where(degree <= WAVES - 1, ordered, 0.0).astype(BF16)

    def spread_rows(shape, row_dim):
        row = iota(shape, row_dim)
        return iota(shape, 1 - row_dim) == 4 * (row >> 4) + (row & 3)

    tall = spread_rows((256, LEVELS), 0).astype(F32).astype(BF16)
    wide = spread_rows((LEVELS, 256), 1).astype(F32).astype(BF16)
    same = ((iota((256, 256), 0) >> 2) & 3) == ((iota((256, 256), 1) >> 2) & 3)
    for part, modes in enumerate(split(modes_ref[...])):
        full = dot(tall, dot(modes, wide).astype(BF16))
        mode2_ref[256 * part : 256 * (part + 1), :] = jnp.where(same, full, 0.0).astype(BF16)
        full = dot(tall, dot_tn(modes, wide).astype(BF16))
        mode1_ref[256 * part : 256 * (part + 1), :] = jnp.where(same, full, 0.0).astype(BF16)

    rate = jnp.sum(
        jnp.where(spread_rows((256, LEVELS), 0), jnp.broadcast_to(rates_ref[...], (256, LEVELS)), 0.0),
        axis=1, keepdims=True,
    )
    rate = jnp.broadcast_to(rate, (256, 128))

    def damp_step(step, carry):
        e = step // 4
        chunk = step % 4
        wave = jnp.where(e == 0, wave_0, wave_1)
        degree = wave + ((iota((256, 128), 0) >> 2) & 1) + 2 * (iota((256, 128), 1) + 128 * chunk)
        degree = degree.astype(F32)
        term = degree * (degree + 1.0) * (IMPLICIT_FACTOR / (WAVES * (WAVES - 1)))
        stiffness = term * rate
        damp_ref[e, chunk] = stiffness / (1.0 + stiffness)
        return carry

    lax.fori_loop(0, 8, damp_step, 0)

    sent_1.wait_recv()

    rows_ref[...] = r1_ref[...].reshape(8 * NB, 128).astype(F32)
    for a in range(2):
        block = stack([rows_ref[pl.ds(4 * a + j, NB, stride=8), :] for j in range(4)]).T.astype(BF16)
        for t in range(8):
            s2_ref[2 * t + a] = block[16 * t : 16 * (t + 1)]
    r2_ref[lev] = s2_ref[lev]
    sent_2 = send_lev(s2_ref, r2_ref, 1)
    sent_2.wait_recv()

    data = r2_ref[...].reshape(256, 128)
    parity = (iota((256, 128), 0) >> 2) & 1
    side = iota((256, 128), 1) >> 6

    def chosen(q, e):
        return ((parity == q) & (side == e)).astype(F32).astype(BF16)

    for step in range(2):
        for e in range(2):
            columns = slice(256 * step, 256 * (step + 1))
            left = jnp.concatenate([data * chosen(0, e), data * chosen(1, e)], axis=1)
            spectral = dot(left, leg_ref[:, columns])
            high, low = split(spectral)
            both = dot(mode1_ref[...], high)
            modal = both[:256] + both[256:] + dot(mode1_ref[:256], low)
            damping = jnp.concatenate([damp_ref[e, 2 * step], damp_ref[e, 2 * step + 1]], axis=1)
            high, low = split(modal * damping)
            both = dot(mode2_ref[...], high)
            change = both[:256] + both[256:] + dot(mode2_ref[:256], low)
            solved_ref[e, :, columns] = (spectral - change).astype(BF16)

    picked = []
    for e in range(2):
        back = dot_nt(solved_ref[e], leg_ref[...])
        picked.append(jnp.where(parity == 0, back[:, :128], back[:, 128:]))
    s3_ref[...] = jnp.where(side == 0, picked[0], picked[1]).astype(BF16).reshape(NL, 16, 128)
    r3_ref[lev] = s3_ref[lev]
    sent_3 = send_lev(s3_ref, r3_ref, 2)
    sent_3.wait_recv()

    for a in range(2):
        block = stack([r3_ref[2 * t + a] for t in range(8)]).astype(F32).T
        for j in range(4):
            rows_ref[pl.ds(4 * a + j, NB, stride=8), :] = block[NB * j : NB * (j + 1)]
    s4_ref[...] = rows_ref[...].astype(BF16).reshape(NB, 8, 128)
    r4_ref[blk] = s4_ref[blk]
    sent_4 = send_blk(s4_ref, r4_ref, 3)
    out_ref[:, :, :, pl.ds(LIVE, PSLOT - LIVE)] = jnp.zeros((2, 2, 4, PSLOT - LIVE), F32)
    sent_4.wait_recv()

    rows_ref[...] = r4_ref[...].reshape(8 * NB, 128).astype(F32)
    for i in range(2):
        four_ref[i] = stack([rows_ref[pl.ds(2 * a + i, NB, stride=8), :] for a in range(4)]).T

    def turn_step(step, carry):
        i = step // TILES
        tile = step % TILES
        wave = wave_ref[tile]
        double = jnp.where(wave == 0.0, 1.0, 2.0)
        start = pl.multiple_of(16 * tile, 16)
        real = four_ref[i, pl.ds(start, 8), :] * double
        imag = four_ref[i, pl.ds(start + 8, 8), :] * double
        for k in range(BLOCKS // 2):
            reals, imags = [], []
            for u in (2 * k, 2 * k + 1):
                c = turn_ref[i, tile, 0, u]
                s = turn_ref[i, tile, 1, u]
                reals.append(real * c + imag * s)
                imags.append(imag * c - real * s)
            for part, rows in enumerate((reals, imags)):
                high, low = split(stack(rows))
                lanes = pl.ds(pl.multiple_of(256 * tile + 128 * part, 128), 128)
                turned_ref[i, 16 * k : 16 * k + 16, lanes] = high
                turned_ref[i, ROWS + 16 * k : ROWS + 16 * k + 16, lanes] = low
        return carry

    lax.fori_loop(0, 2 * TILES, turn_step, 0)

    for i in range(2):
        both = dot_nt(turned_ref[i], table_ref[i])
        points = points_of(i)
        for u in range(BLOCKS):
            value = both[8 * u : 8 * u + 8] + both[ROWS + 8 * u : ROWS + 8 * u + 8]
            live = iota((4, SPAN), 1) + SPAN * u < points
            out_ref[i, 0, :, SPAN * u : SPAN * (u + 1)] = jnp.where(live, value[:4] + value[4:], 0.0)
            out_ref[i, 1, :, SPAN * u : SPAN * (u + 1)] = jnp.where(live, value[:4] - value[4:], 0.0)

    for sent in (sent_1, sent_2, sent_3, sent_4):
        sent.wait_send()


def shards(grid_values, quad_weight, legendre, vertical_modes, eigenvalues, pair_latitude, wave_slot):
    vmem = pl.BlockSpec(memory_space=pltpu.VMEM)
    smem = pl.BlockSpec(memory_space=pltpu.SMEM)
    hbm = pl.BlockSpec(memory_space=pl.ANY)
    return pl.pallas_call(
        kernel,
        out_shape=pltpu.VMEM(grid_values.shape, F32),
        in_specs=[hbm, smem, hbm, vmem, vmem, smem, vmem, smem],
        out_specs=vmem,
        scratch_shapes=[
            pltpu.VMEM((2, 2, 4, PSLOT), F32),
            pltpu.VMEM((2, 2, 64, HALF), BF16),
            pltpu.VMEM((TILES, 8, 128), F32),
            pltpu.VMEM((2, 2, ROWS, SPAN), BF16),
            pltpu.VMEM((2, SPAN, 2 * WAVES), BF16),
            pltpu.VMEM((2, TILES, 2, BLOCKS, 8, 128), F32),
            pltpu.VMEM((2, 128, 128), F32),
            pltpu.VMEM((8 * NB, 128), F32),
            pltpu.VMEM((NB, 8, 128), BF16),
            pltpu.VMEM((NB, 8, 128), BF16),
            pltpu.VMEM((NL, 16, 128), BF16),
            pltpu.VMEM((NL, 16, 128), BF16),
            pltpu.VMEM((NL, 16, 128), BF16),
            pltpu.VMEM((NL, 16, 128), BF16),
            pltpu.VMEM((NB, 8, 128), BF16),
            pltpu.VMEM((NB, 8, 128), BF16),
            pltpu.VMEM((256, HALF), BF16),
            pltpu.VMEM((512, 256), BF16),
            pltpu.VMEM((512, 256), BF16),
            pltpu.VMEM((2, 4, 256, 128), F32),
            pltpu.VMEM((2, 256, HALF), BF16),
            pltpu.VMEM((2, 2 * ROWS, 2 * WAVES), BF16),
            pltpu.SemaphoreType.DMA((2,)),
            pltpu.SemaphoreType.DMA((4,)),
            pltpu.SemaphoreType.DMA((4,)),
        ],
        compiler_params=pltpu.CompilerParams(
            collective_id=0, has_side_effects=True, vmem_limit_bytes=60 * 1024 * 1024
        ),
        cost_estimate=pl.CostEstimate(flops=4_000_000_000, bytes_accessed=1_500_000, transcendentals=0),
    )(
        grid_values, quad_weight, legendre, vertical_modes, eigenvalues.reshape(1, LEVELS),
        pair_latitude, wave_slot.reshape(8, 128), wave_slot,
    )


def solution(mesh):
    in_specs = (
        P("blk", None, "lev", None),
        P("blk"),
        P("blk", None, None, None),
        P(),
        P(),
        P("blk"),
        P(),
    )
    out_specs = P("blk", None, "lev", None)
    return jax.shard_map(shards, mesh=mesh, in_specs=in_specs, out_specs=out_specs, check_vma=False)
```

```python
import jax
import jax.numpy as jnp
from jax import lax
from jax.experimental import pallas as pl
from jax.experimental.pallas import tpu as pltpu
from jax.sharding import PartitionSpec as P

MESH = pl.DeviceIdType.MESH
BF16 = jnp.bfloat16
F32 = jnp.float32

WAVES = 1024
HALF = 512
LEVELS = 64
NB = 32
NL = 16
SPAN = 256
BLOCKS = 22
ROWS = 8 * BLOCKS
TILES = WAVES // 128
LIVE = BLOCKS * SPAN
PSLOT = 6144
IMPLICIT_FACTOR = 4.0
PI = 3.141592653589793


def ring(step, size):
    return min(step, size - step)


BLK_PEERS = sorted(
    [(y, x) for y in range(8) for x in range(4) if (y, x) != (0, 0)],
    key=lambda d: (-ring(d[0], 8) - ring(d[1], 4), d),
)
LEV_PEERS = sorted(
    [(z, c) for z in range(8) for c in range(2) if (z, c) != (0, 0)],
    key=lambda d: (-ring(d[0], 8) - 0.5 * d[1], d),
)


def blk_peer(blk, peer):
    return (blk // 4 + peer[0]) % 8 * 4 + (blk % 4 + peer[1]) % 4


def lev_peer(lev, peer):
    return (lev // 2 + peer[0]) % 8 * 2 + (lev % 2 + peer[1]) % 2


def iota(shape, dim):
    return lax.broadcasted_iota(jnp.int32, shape, dim)


def dot(a, b):
    return jnp.dot(a, b, preferred_element_type=F32)


def dot_nt(a, b):
    return lax.dot_general(a, b, (((1,), (1,)), ((), ())), preferred_element_type=F32)


def dot_tn(a, b):
    return lax.dot_general(a, b, (((0,), (0,)), ((), ())), preferred_element_type=F32)


def split(x):
    high = x.astype(BF16)
    return high, (x - high.astype(F32)).astype(BF16)


def rotation(phase, points, inverse):
    turns = jnp.floor(phase * inverse + 0.5)
    x = (phase - turns * points) * inverse
    z = x * x
    sine = 0.0
    cosine = 0.0
    sin_terms = [PI]
    cos_terms = [1.0]
    for k in range(1, 7):
        sin_terms.append(-sin_terms[-1] * PI * PI / ((2 * k) * (2 * k + 1)))
        cos_terms.append(-cos_terms[-1] * PI * PI / ((2 * k - 1) * (2 * k)))
    sine = jnp.full_like(z, sin_terms[6])
    cosine = jnp.full_like(z, cos_terms[6])
    for k in range(5, -1, -1):
        sine = sine * z + sin_terms[k]
        cosine = cosine * z + cos_terms[k]
    sine = sine * x
    return 1.0 - 2.0 * sine * sine, -2.0 * sine * cosine


def turn(a, b):
    return a[0] * b[0] - a[1] * b[1], a[0] * b[1] + a[1] * b[0]


def stack(parts):
    return jnp.concatenate(parts, axis=0)


def kernel(
    grid_hbm, weight_ref, legendre_hbm, modes_ref, rates_ref, cycle_ref, slot_ref, slot_smem,
    out_ref,
    grid_ref, raw_ref, wave_ref, x_ref, table_ref, rest_ref, turn_ref, four_ref,
    rows_ref, s1_ref, r1_ref, s2_ref, r2_ref, s3_ref, r3_ref, s4_ref, r4_ref,
    leg_ref, mode1_ref, mode2_ref, damp_ref, solved_ref,
    load_sem, send_sem, recv_sem,
):
    blk = lax.axis_index("blk")
    lev = lax.axis_index("lev")

    barrier = pltpu.get_barrier_semaphore()

    grid_copy = pltpu.make_async_copy(grid_hbm, grid_ref, load_sem.at[0])
    grid_copy.start()
    legendre_copy = pltpu.make_async_copy(
        legendre_hbm.at[pl.ds(2 * lev, 2)], raw_ref, load_sem.at[1]
    )
    legendre_copy.start()
    for peer in BLK_PEERS:
        pl.semaphore_signal(barrier, inc=1, device_id=(blk_peer(blk, peer), lev), device_id_type=MESH)
    for peer in LEV_PEERS:
        pl.semaphore_signal(barrier, inc=1, device_id=(blk, lev_peer(lev, peer)), device_id_type=MESH)

    column = iota((128, WAVES), 1)
    pick = (iota((128, WAVES), 0) == 32 * (column & 3) + (column >> 5)).astype(F32).astype(BF16)
    slots = slot_ref[...]
    halves = stack([slots >> 5, slots & 31]).astype(F32).astype(BF16)
    spread = dot(halves, pick)
    column = iota((8, WAVES), 1)
    mine = iota((8, WAVES), 0) == ((column & 31) >> 2)
    spread = jnp.where(mine, 32.0 * spread[:8] + spread[8:], 0.0)
    waves = jnp.sum(spread, axis=0, keepdims=True)
    for tile in range(TILES):
        wave_ref[tile] = jnp.broadcast_to(waves[:, 128 * tile : 128 * (tile + 1)], (8, 128))

    def points_of(i):
        return 20 + 4 * cycle_ref[i]

    def rotations(i, tile):
        points = jnp.full((8, 128), points_of(i), jnp.int32).astype(F32)
        inverse = 1.0 / points
        wave = wave_ref[tile]
        row = iota((8, 128), 0)
        place = row.astype(F32)
        extra = jnp.where(row == 0, 8.0, jnp.where(row == 1, 128.0, 2048.0))
        fine = rotation(place * wave, points, inverse)
        coarse = rotation(16.0 * place * wave, points, inverse)
        block = rotation(256.0 * place * wave, points, inverse)
        jump = rotation(extra * wave, points, inverse)

        def spread_row(pair, k):
            return tuple(jnp.broadcast_to(part[k : k + 1], (8, 128)) for part in pair)

        fine_next = turn(fine, spread_row(jump, 0))
        coarse_next = turn(coarse, spread_row(jump, 1))
        leap = spread_row(jump, 2)
        kept = (2.0 * wave < points).astype(F32)
        block = (block[0] * kept, block[1] * kept)
        block_1 = turn(block, leap)
        block_2 = turn(block_1, leap)

        high = [[], []]
        low = [[], []]
        for a in range(16):
            lead = spread_row(coarse if a < 8 else coarse_next, a % 8)
            first = turn(lead, fine)
            second = turn(lead, fine_next)
            for part in range(2):
                h, l = split(stack([first[part], second[part]]))
                high[part].append(h)
                low[part].append(l)
        table = jnp.concatenate([stack(high[0]), stack(high[1])], axis=1)
        rest = jnp.concatenate([stack(low[0]), stack(low[1])], axis=1)
        table_ref[i, :, pl.ds(pl.multiple_of(256 * tile, 256), 256)] = table
        turns = [spread_row((block, block_1, block_2)[u // 8], u % 8) for u in range(BLOCKS)]
        for u in range(BLOCKS):
            turn_ref[i, tile, 0, u], turn_ref[i, tile, 1, u] = turns[u]
        return table, rest, turns

    def transform(i, tile, table, rest, turns):
        x_high = x_ref[i, 0]
        sums = dot(
            jnp.concatenate([x_high, x_ref[i, 1], x_high], axis=1),
            jnp.concatenate([table, table, rest], axis=0),
        )
        real = jnp.zeros((8, 128), F32)
        imag = jnp.zeros((8, 128), F32)
        for u in range(BLOCKS):
            c, s = turns[u]
            p, q = sums[8 * u : 8 * u + 8, :128], sums[8 * u : 8 * u + 8, 128:]
            real = real + (c * p - s * q)
            imag = imag + (c * q + s * p)
        start = pl.multiple_of(16 * tile, 16)
        four_ref[i, pl.ds(start, 8), :] = real
        four_ref[i, pl.ds(start + 8, 8), :] = imag

    def early_step(tile, carry):
        _, rest, _ = rotations(0, tile)
        rest_ref[:, pl.ds(pl.multiple_of(256 * tile, 256), 256)] = rest
        return carry

    lax.fori_loop(0, 8, early_step, 0, unroll=8)

    grid_copy.wait()

    def fold_step(step, carry):
        i = step // (BLOCKS // 2)
        k = step % (BLOCKS // 2)
        points = points_of(i)
        scale = jnp.full((4, SPAN), weight_ref[i], F32) / jnp.full((4, SPAN), points, jnp.int32).astype(F32)
        rows = []
        for half in range(2):
            start = pl.multiple_of(512 * k + 256 * half, 256)
            live = iota((4, SPAN), 1) + start < points
            north = grid_ref[i, 0, :, pl.ds(start, SPAN)]
            south = grid_ref[i, 1, :, pl.ds(start, SPAN)]
            rows.append(jnp.where(live, (north + south) * scale, 0.0))
            rows.append(jnp.where(live, (north - south) * scale, 0.0))
        high, low = split(stack(rows))
        x_ref[i, 0, pl.ds(pl.multiple_of(16 * k, 16), 16), :] = high
        x_ref[i, 1, pl.ds(pl.multiple_of(16 * k, 16), 16), :] = low
        return carry

    lax.fori_loop(0, BLOCKS, fold_step, 0, unroll=2)

    def early_transform(tile, carry):
        lanes = pl.ds(pl.multiple_of(256 * tile, 256), 256)
        turns = [(turn_ref[0, tile, 0, u], turn_ref[0, tile, 1, u]) for u in range(BLOCKS)]
        transform(0, tile, table_ref[0, :, lanes], rest_ref[:, lanes], turns)
        return carry

    def analyse_step(step, carry):
        transform(step // TILES, step % TILES, *rotations(step // TILES, step % TILES))
        return carry

    lax.fori_loop(0, 8, early_transform, 0, unroll=8)
    lax.fori_loop(8, 2 * TILES, analyse_step, 0, unroll=8)

    for i in range(2):
        flipped = four_ref[i].T
        for a in range(4):
            rows_ref[pl.ds(2 * a + i, NB, stride=8), :] = flipped[NB * a : NB * (a + 1)]
    s1_ref[...] = rows_ref[...].astype(BF16).reshape(NB, 8, 128)
    r1_ref[blk] = s1_ref[blk]
    pl.semaphore_wait(barrier, NB + NL - 2)

    def send_blk(source, target, sem):
        for peer in BLK_PEERS:
            other = blk_peer(blk, peer)
            pltpu.make_async_remote_copy(
                src_ref=source.at[other],
                dst_ref=target.at[blk],
                send_sem=send_sem.at[sem],
                recv_sem=recv_sem.at[sem],
                device_id=(other, lev),
                device_id_type=MESH,
            ).start()
        rows = pl.ds(0, NB - 1)
        return pltpu.make_async_remote_copy(
            src_ref=source.at[rows], dst_ref=target.at[rows],
            send_sem=send_sem.at[sem], recv_sem=recv_sem.at[sem],
            device_id=(blk_peer(blk, BLK_PEERS[0]), lev), device_id_type=MESH,
        )

    def send_lev(source, target, sem):
        for peer in LEV_PEERS:
            other = lev_peer(lev, peer)
            pltpu.make_async_remote_copy(
                src_ref=source.at[other],
                dst_ref=target.at[lev],
                send_sem=send_sem.at[sem],
                recv_sem=recv_sem.at[sem],
                device_id=(blk, other),
                device_id_type=MESH,
            ).start()
        rows = pl.ds(0, NL - 1)
        return pltpu.make_async_remote_copy(
            src_ref=source.at[rows], dst_ref=target.at[rows],
            send_sem=send_sem.at[sem], recv_sem=recv_sem.at[sem],
            device_id=(blk, lev_peer(lev, LEV_PEERS[0])), device_id_type=MESH,
        )

    sent_1 = send_blk(s1_ref, r1_ref, 0)

    legendre_copy.wait()
    wave_0 = slot_smem[32 * blk + 2 * lev]
    wave_1 = slot_smem[32 * blk + 2 * lev + 1]
    row = iota((256, 256), 0)
    source = ((row >> 6) & 1) * 128 + (row >> 7) * 64 + 2 * (row & 31) + ((row >> 5) & 1)
    reorder = (iota((256, 256), 1) == source).astype(F32).astype(BF16)
    ordered = dot(reorder, raw_ref[...].reshape(256, HALF))
    row = iota((256, HALF), 0)
    degree = jnp.where(((row >> 6) & 1) == 0, wave_0, wave_1) + (row >> 7) + 2 * iota((256, HALF), 1)
    leg_ref[...] = jnp.where(degree <= WAVES - 1, ordered, 0.0).astype(BF16)

    def spread_rows(shape, row_dim):
        row = iota(shape, row_dim)
        return iota(shape, 1 - row_dim) == 4 * (row >> 4) + (row & 3)

    tall = spread_rows((256, LEVELS), 0).astype(F32).astype(BF16)
    wide = spread_rows((LEVELS, 256), 1).astype(F32).astype(BF16)
    same = ((iota((256, 256), 0) >> 2) & 3) == ((iota((256, 256), 1) >> 2) & 3)
    for part, modes in enumerate(split(modes_ref[...])):
        full = dot(tall, dot(modes, wide).astype(BF16))
        mode2_ref[256 * part : 256 * (part + 1), :] = jnp.where(same, full, 0.0).astype(BF16)
        full = dot(tall, dot_tn(modes, wide).astype(BF16))
        mode1_ref[256 * part : 256 * (part + 1), :] = jnp.where(same, full, 0.0).astype(BF16)

    rate = jnp.sum(
        jnp.where(spread_rows((256, LEVELS), 0), jnp.broadcast_to(rates_ref[...], (256, LEVELS)), 0.0),
        axis=1, keepdims=True,
    )
    rate = jnp.broadcast_to(rate, (256, 128))

    def damp_step(step, carry):
        e = step // 4
        chunk = step % 4
        wave = jnp.where(e == 0, wave_0, wave_1)
        degree = wave + ((iota((256, 128), 0) >> 2) & 1) + 2 * (iota((256, 128), 1) + 128 * chunk)
        degree = degree.astype(F32)
        term = degree * (degree + 1.0) * (IMPLICIT_FACTOR / (WAVES * (WAVES - 1)))
        stiffness = term * rate
        damp_ref[e, chunk] = stiffness / (1.0 + stiffness)
        return carry

    lax.fori_loop(0, 8, damp_step, 0)

    sent_1.wait_recv()

    rows_ref[...] = r1_ref[...].reshape(8 * NB, 128).astype(F32)
    for a in range(2):
        block = stack([rows_ref[pl.ds(4 * a + j, NB, stride=8), :] for j in range(4)]).T.astype(BF16)
        for t in range(8):
            s2_ref[2 * t + a] = block[16 * t : 16 * (t + 1)]
    r2_ref[lev] = s2_ref[lev]
    sent_2 = send_lev(s2_ref, r2_ref, 1)
    sent_2.wait_recv()

    data = r2_ref[...].reshape(256, 128)
    parity = (iota((256, 128), 0) >> 2) & 1
    side = iota((256, 128), 1) >> 6

    def chosen(q, e):
        return ((parity == q) & (side == e)).astype(F32).astype(BF16)

    for step in range(2):
        for e in range(2):
            columns = slice(256 * step, 256 * (step + 1))
            left = jnp.concatenate([data * chosen(0, e), data * chosen(1, e)], axis=1)
            spectral = dot(left, leg_ref[:, columns])
            both = dot(mode1_ref[...], spectral.astype(BF16))
            modal = both[:256] + both[256:]
            damping = jnp.concatenate([damp_ref[e, 2 * step], damp_ref[e, 2 * step + 1]], axis=1)
            both = dot(mode2_ref[...], (modal * damping).astype(BF16))
            change = both[:256] + both[256:]
            solved_ref[e, :, columns] = (spectral - change).astype(BF16)

    picked = []
    for e in range(2):
        back = dot_nt(solved_ref[e], leg_ref[...])
        picked.append(jnp.where(parity == 0, back[:, :128], back[:, 128:]))
    s3_ref[...] = jnp.where(side == 0, picked[0], picked[1]).astype(BF16).reshape(NL, 16, 128)
    r3_ref[lev] = s3_ref[lev]
    sent_3 = send_lev(s3_ref, r3_ref, 2)
    sent_3.wait_recv()

    for a in range(2):
        block = stack([r3_ref[2 * t + a] for t in range(8)]).astype(F32).T
        for j in range(4):
            rows_ref[pl.ds(4 * a + j, NB, stride=8), :] = block[NB * j : NB * (j + 1)]
    s4_ref[...] = rows_ref[...].astype(BF16).reshape(NB, 8, 128)
    r4_ref[blk] = s4_ref[blk]
    sent_4 = send_blk(s4_ref, r4_ref, 3)
    out_ref[:, :, :, pl.ds(LIVE, PSLOT - LIVE)] = jnp.zeros((2, 2, 4, PSLOT - LIVE), F32)
    sent_4.wait_recv()

    rows_ref[...] = r4_ref[...].reshape(8 * NB, 128).astype(F32)
    for i in range(2):
        four_ref[i] = stack([rows_ref[pl.ds(2 * a + i, NB, stride=8), :] for a in range(4)]).T

    for i in range(2):
        points = points_of(i)
        value = 0.0
        for group in range(2):
            left = []
            for tile in range(4 * group, 4 * group + 4):
                double = jnp.where(wave_ref[tile] == 0.0, 1.0, 2.0)
                real = four_ref[i, 16 * tile : 16 * tile + 8, :] * double
                imag = four_ref[i, 16 * tile + 8 : 16 * tile + 16, :] * double
                reals, imags = [], []
                for u in range(BLOCKS):
                    c = turn_ref[i, tile, 0, u]
                    s = turn_ref[i, tile, 1, u]
                    reals.append(real * c + imag * s)
                    imags.append(imag * c - real * s)
                left += [stack(reals).astype(BF16), stack(imags).astype(BF16)]
            right = table_ref[i, :, 1024 * group : 1024 * (group + 1)]
            value = value + dot_nt(jnp.concatenate(left, axis=1), right)
        for u in range(BLOCKS):
            even = value[8 * u : 8 * u + 4]
            odd = value[8 * u + 4 : 8 * u + 8]
            live = iota((4, SPAN), 1) + SPAN * u < points
            out_ref[i, 0, :, SPAN * u : SPAN * (u + 1)] = jnp.where(live, even + odd, 0.0)
            out_ref[i, 1, :, SPAN * u : SPAN * (u + 1)] = jnp.where(live, even - odd, 0.0)

    for sent in (sent_1, sent_2, sent_3, sent_4):
        sent.wait_send()


def shards(grid_values, quad_weight, legendre, vertical_modes, eigenvalues, pair_latitude, wave_slot):
    vmem = pl.BlockSpec(memory_space=pltpu.VMEM)
    smem = pl.BlockSpec(memory_space=pltpu.SMEM)
    hbm = pl.BlockSpec(memory_space=pl.ANY)
    return pl.pallas_call(
        kernel,
        out_shape=pltpu.VMEM(grid_values.shape, F32),
        in_specs=[hbm, smem, hbm, vmem, vmem, smem, vmem, smem],
        out_specs=vmem,
        scratch_shapes=[
            pltpu.VMEM((2, 2, 4, PSLOT), F32),
            pltpu.VMEM((2, 2, 64, HALF), BF16),
            pltpu.VMEM((TILES, 8, 128), F32),
            pltpu.VMEM((2, 2, ROWS, SPAN), BF16),
            pltpu.VMEM((2, SPAN, 2 * WAVES), BF16),
            pltpu.VMEM((SPAN, 2 * WAVES), BF16),
            pltpu.VMEM((2, TILES, 2, BLOCKS, 8, 128), F32),
            pltpu.VMEM((2, 128, 128), F32),
            pltpu.VMEM((8 * NB, 128), F32),
            pltpu.VMEM((NB, 8, 128), BF16),
            pltpu.VMEM((NB, 8, 128), BF16),
            pltpu.VMEM((NL, 16, 128), BF16),
            pltpu.VMEM((NL, 16, 128), BF16),
            pltpu.VMEM((NL, 16, 128), BF16),
            pltpu.VMEM((NL, 16, 128), BF16),
            pltpu.VMEM((NB, 8, 128), BF16),
            pltpu.VMEM((NB, 8, 128), BF16),
            pltpu.VMEM((256, HALF), BF16),
            pltpu.VMEM((512, 256), BF16),
            pltpu.VMEM((512, 256), BF16),
            pltpu.VMEM((2, 4, 256, 128), F32),
            pltpu.VMEM((2, 256, HALF), BF16),
            pltpu.SemaphoreType.DMA((2,)),
            pltpu.SemaphoreType.DMA((4,)),
            pltpu.SemaphoreType.DMA((4,)),
        ],
        compiler_params=pltpu.CompilerParams(
            collective_id=0, has_side_effects=True, vmem_limit_bytes=60 * 1024 * 1024
        ),
        cost_estimate=pl.CostEstimate(flops=4_000_000_000, bytes_accessed=1_500_000, transcendentals=0),
    )(
        grid_values, quad_weight, legendre, vertical_modes, eigenvalues.reshape(1, LEVELS),
        pair_latitude, wave_slot.reshape(8, 128), wave_slot,
    )


def solution(mesh):
    in_specs = (
        P("blk", None, "lev", None),
        P("blk"),
        P("blk", None, None, None),
        P(),
        P(),
        P("blk"),
        P(),
    )
    out_specs = P("blk", None, "lev", None)
    return jax.shard_map(shards, mesh=mesh, in_specs=in_specs, out_specs=out_specs, check_vma=False)
```

```python
import jax
import jax.numpy as jnp
from jax import lax
from jax.experimental import pallas as pl
from jax.experimental.pallas import tpu as pltpu
from jax.sharding import PartitionSpec as P

MESH = pl.DeviceIdType.MESH
BF16 = jnp.bfloat16
F32 = jnp.float32

WAVES = 1024
HALF = 512
LEVELS = 64
NB = 32
NL = 16
SPAN = 256
BLOCKS = 22
ROWS = 8 * BLOCKS
TILES = WAVES // 128
LIVE = BLOCKS * SPAN
PSLOT = 6144
IMPLICIT_FACTOR = 4.0
PI = 3.141592653589793


def ring(step, size):
    return min(step, size - step)


BLK_PEERS = sorted(
    [(y, x) for y in range(8) for x in range(4) if (y, x) != (0, 0)],
    key=lambda d: (-ring(d[0], 8) - ring(d[1], 4), d),
)
LEV_PEERS = sorted(
    [(z, c) for z in range(8) for c in range(2) if (z, c) != (0, 0)],
    key=lambda d: (-ring(d[0], 8) - 0.5 * d[1], d),
)


def blk_peer(blk, peer):
    return (blk // 4 + peer[0]) % 8 * 4 + (blk % 4 + peer[1]) % 4


def lev_peer(lev, peer):
    return (lev // 2 + peer[0]) % 8 * 2 + (lev % 2 + peer[1]) % 2


def iota(shape, dim):
    return lax.broadcasted_iota(jnp.int32, shape, dim)


def dot(a, b):
    return jnp.dot(a, b, preferred_element_type=F32)


def dot_nt(a, b):
    return lax.dot_general(a, b, (((1,), (1,)), ((), ())), preferred_element_type=F32)


def dot_tn(a, b):
    return lax.dot_general(a, b, (((0,), (0,)), ((), ())), preferred_element_type=F32)


def split(x):
    high = x.astype(BF16)
    return high, (x - high.astype(F32)).astype(BF16)


def rotation(phase, points, inverse):
    turns = jnp.floor(phase * inverse + 0.5)
    x = (phase - turns * points) * inverse
    z = x * x
    sine = 0.0
    cosine = 0.0
    sin_terms = [PI]
    cos_terms = [1.0]
    for k in range(1, 7):
        sin_terms.append(-sin_terms[-1] * PI * PI / ((2 * k) * (2 * k + 1)))
        cos_terms.append(-cos_terms[-1] * PI * PI / ((2 * k - 1) * (2 * k)))
    sine = jnp.full_like(z, sin_terms[6])
    cosine = jnp.full_like(z, cos_terms[6])
    for k in range(5, -1, -1):
        sine = sine * z + sin_terms[k]
        cosine = cosine * z + cos_terms[k]
    sine = sine * x
    return 1.0 - 2.0 * sine * sine, -2.0 * sine * cosine


def turn(a, b):
    return a[0] * b[0] - a[1] * b[1], a[0] * b[1] + a[1] * b[0]


def stack(parts):
    return jnp.concatenate(parts, axis=0)


def kernel(
    grid_hbm, weight_ref, legendre_hbm, modes_ref, rates_ref, cycle_ref, slot_ref, slot_smem,
    out_ref,
    grid_ref, raw_ref, wave_ref, x_ref, table_ref, rest_ref, flip_ref, turn_ref, four_ref,
    rows_ref, s1_ref, r1_ref, s2_ref, r2_ref, s3_ref, r3_ref, s4_ref, r4_ref,
    leg_ref, mode1_ref, mode2_ref, damp_ref, solved_ref,
    load_sem, send_sem, recv_sem,
):
    blk = lax.axis_index("blk")
    lev = lax.axis_index("lev")

    barrier = pltpu.get_barrier_semaphore()

    grid_copy = pltpu.make_async_copy(grid_hbm, grid_ref, load_sem.at[0])
    grid_copy.start()
    legendre_copy = pltpu.make_async_copy(
        legendre_hbm.at[pl.ds(2 * lev, 2)], raw_ref, load_sem.at[1]
    )
    legendre_copy.start()
    for peer in BLK_PEERS:
        pl.semaphore_signal(barrier, inc=1, device_id=(blk_peer(blk, peer), lev), device_id_type=MESH)
    for peer in LEV_PEERS:
        pl.semaphore_signal(barrier, inc=1, device_id=(blk, lev_peer(lev, peer)), device_id_type=MESH)

    column = iota((128, WAVES), 1)
    pick = (iota((128, WAVES), 0) == 32 * (column & 3) + (column >> 5)).astype(F32).astype(BF16)
    slots = slot_ref[...]
    halves = stack([slots >> 5, slots & 31]).astype(F32).astype(BF16)
    spread = dot(halves, pick)
    column = iota((8, WAVES), 1)
    mine = iota((8, WAVES), 0) == ((column & 31) >> 2)
    spread = jnp.where(mine, 32.0 * spread[:8] + spread[8:], 0.0)
    waves = jnp.sum(spread, axis=0, keepdims=True)
    for tile in range(TILES):
        wave_ref[tile] = jnp.broadcast_to(waves[:, 128 * tile : 128 * (tile + 1)], (8, 128))

    def points_of(i):
        return 20 + 4 * cycle_ref[i]

    def rotations(i, tile):
        points = jnp.full((8, 128), points_of(i), jnp.int32).astype(F32)
        inverse = 1.0 / points
        wave = wave_ref[tile]
        row = iota((8, 128), 0)
        place = row.astype(F32)
        extra = jnp.where(row == 0, 8.0, jnp.where(row == 1, 128.0, 2048.0))
        fine = rotation(place * wave, points, inverse)
        coarse = rotation(16.0 * place * wave, points, inverse)
        block = rotation(256.0 * place * wave, points, inverse)
        jump = rotation(extra * wave, points, inverse)

        def spread_row(pair, k):
            return tuple(jnp.broadcast_to(part[k : k + 1], (8, 128)) for part in pair)

        fine_next = turn(fine, spread_row(jump, 0))
        coarse_next = turn(coarse, spread_row(jump, 1))
        leap = spread_row(jump, 2)
        kept = (2.0 * wave < points).astype(F32)
        block = (block[0] * kept, block[1] * kept)
        block_1 = turn(block, leap)
        block_2 = turn(block_1, leap)

        high = [[], []]
        low = [[], []]
        for a in range(16):
            lead = spread_row(coarse if a < 8 else coarse_next, a % 8)
            first = turn(lead, fine)
            second = turn(lead, fine_next)
            for part in range(2):
                h, l = split(stack([first[part], second[part]]))
                high[part].append(h)
                low[part].append(l)
        table = jnp.concatenate([stack(high[0]), stack(high[1])], axis=1)
        rest = jnp.concatenate([stack(low[0]), stack(low[1])], axis=1)
        table_ref[i, :, pl.ds(pl.multiple_of(256 * tile, 256), 256)] = table
        turns = [spread_row((block, block_1, block_2)[u // 8], u % 8) for u in range(BLOCKS)]
        for u in range(BLOCKS):
            turn_ref[i, tile, 0, u], turn_ref[i, tile, 1, u] = turns[u]
        return table, rest, turns

    def transform(i, tile, table, rest, turns):
        x_high = x_ref[i, 0]
        sums = dot(
            jnp.concatenate([x_high, x_ref[i, 1], x_high], axis=1),
            jnp.concatenate([table, table, rest], axis=0),
        )
        real = jnp.zeros((8, 128), F32)
        imag = jnp.zeros((8, 128), F32)
        for u in range(BLOCKS):
            c, s = turns[u]
            p, q = sums[8 * u : 8 * u + 8, :128], sums[8 * u : 8 * u + 8, 128:]
            real = real + (c * p - s * q)
            imag = imag + (c * q + s * p)
        start = pl.multiple_of(16 * tile, 16)
        four_ref[i, pl.ds(start, 8), :] = real
        four_ref[i, pl.ds(start + 8, 8), :] = imag

    def early_step(tile, carry):
        _, rest, _ = rotations(0, tile)
        rest_ref[:, pl.ds(pl.multiple_of(256 * tile, 256), 256)] = rest
        return carry

    lax.fori_loop(0, 8, early_step, 0, unroll=8)

    grid_copy.wait()

    def fold_step(step, carry):
        i = step // (BLOCKS // 2)
        k = step % (BLOCKS // 2)
        points = points_of(i)
        scale = jnp.full((4, SPAN), weight_ref[i], F32) / jnp.full((4, SPAN), points, jnp.int32).astype(F32)
        rows = []
        for half in range(2):
            start = pl.multiple_of(512 * k + 256 * half, 256)
            live = iota((4, SPAN), 1) + start < points
            north = grid_ref[i, 0, :, pl.ds(start, SPAN)]
            south = grid_ref[i, 1, :, pl.ds(start, SPAN)]
            rows.append(jnp.where(live, (north + south) * scale, 0.0))
            rows.append(jnp.where(live, (north - south) * scale, 0.0))
        high, low = split(stack(rows))
        x_ref[i, 0, pl.ds(pl.multiple_of(16 * k, 16), 16), :] = high
        x_ref[i, 1, pl.ds(pl.multiple_of(16 * k, 16), 16), :] = low
        return carry

    lax.fori_loop(0, BLOCKS, fold_step, 0, unroll=2)

    def early_transform(tile, carry):
        lanes = pl.ds(pl.multiple_of(256 * tile, 256), 256)
        turns = [(turn_ref[0, tile, 0, u], turn_ref[0, tile, 1, u]) for u in range(BLOCKS)]
        transform(0, tile, table_ref[0, :, lanes], rest_ref[:, lanes], turns)
        return carry

    def analyse_step(step, carry):
        transform(step // TILES, step % TILES, *rotations(step // TILES, step % TILES))
        return carry

    lax.fori_loop(0, 8, early_transform, 0, unroll=8)
    lax.fori_loop(8, 2 * TILES, analyse_step, 0, unroll=8)

    for i in range(2):
        flipped = four_ref[i].T
        for a in range(4):
            rows_ref[pl.ds(2 * a + i, NB, stride=8), :] = flipped[NB * a : NB * (a + 1)]
    s1_ref[...] = rows_ref[...].astype(BF16).reshape(NB, 8, 128)
    r1_ref[blk] = s1_ref[blk]
    pl.semaphore_wait(barrier, NB + NL - 2)

    def send_blk(source, target, sem):
        for peer in BLK_PEERS:
            other = blk_peer(blk, peer)
            pltpu.make_async_remote_copy(
                src_ref=source.at[other],
                dst_ref=target.at[blk],
                send_sem=send_sem.at[sem],
                recv_sem=recv_sem.at[sem],
                device_id=(other, lev),
                device_id_type=MESH,
            ).start()
        rows = pl.ds(0, NB - 1)
        return pltpu.make_async_remote_copy(
            src_ref=source.at[rows], dst_ref=target.at[rows],
            send_sem=send_sem.at[sem], recv_sem=recv_sem.at[sem],
            device_id=(blk_peer(blk, BLK_PEERS[0]), lev), device_id_type=MESH,
        )

    def send_lev(source, target, sem):
        for peer in LEV_PEERS:
            other = lev_peer(lev, peer)
            pltpu.make_async_remote_copy(
                src_ref=source.at[other],
                dst_ref=target.at[lev],
                send_sem=send_sem.at[sem],
                recv_sem=recv_sem.at[sem],
                device_id=(blk, other),
                device_id_type=MESH,
            ).start()
        rows = pl.ds(0, NL - 1)
        return pltpu.make_async_remote_copy(
            src_ref=source.at[rows], dst_ref=target.at[rows],
            send_sem=send_sem.at[sem], recv_sem=recv_sem.at[sem],
            device_id=(blk, lev_peer(lev, LEV_PEERS[0])), device_id_type=MESH,
        )

    sent_1 = send_blk(s1_ref, r1_ref, 0)

    legendre_copy.wait()
    wave_0 = slot_smem[32 * blk + 2 * lev]
    wave_1 = slot_smem[32 * blk + 2 * lev + 1]
    row = iota((256, 256), 0)
    source = ((row >> 6) & 1) * 128 + (row >> 7) * 64 + 2 * (row & 31) + ((row >> 5) & 1)
    reorder = (iota((256, 256), 1) == source).astype(F32).astype(BF16)
    ordered = dot(reorder, raw_ref[...].reshape(256, HALF))
    row = iota((256, HALF), 0)
    degree = jnp.where(((row >> 6) & 1) == 0, wave_0, wave_1) + (row >> 7) + 2 * iota((256, HALF), 1)
    leg_ref[...] = jnp.where(degree <= WAVES - 1, ordered, 0.0).astype(BF16)

    def spread_rows(shape, row_dim):
        row = iota(shape, row_dim)
        return iota(shape, 1 - row_dim) == 4 * (row >> 4) + (row & 3)

    tall = spread_rows((256, LEVELS), 0).astype(F32).astype(BF16)
    wide = spread_rows((LEVELS, 256), 1).astype(F32).astype(BF16)
    same = ((iota((256, 256), 0) >> 2) & 3) == ((iota((256, 256), 1) >> 2) & 3)
    modes = modes_ref[...].astype(BF16)
    full = dot(tall, dot(modes, wide).astype(BF16))
    mode2_ref[...] = jnp.where(same, full, 0.0).astype(BF16)
    full = dot(tall, dot_tn(modes, wide).astype(BF16))
    mode1_ref[...] = jnp.where(same, full, 0.0).astype(BF16)

    rate = jnp.sum(
        jnp.where(spread_rows((256, LEVELS), 0), jnp.broadcast_to(rates_ref[...], (256, LEVELS)), 0.0),
        axis=1, keepdims=True,
    )
    rate = jnp.broadcast_to(rate, (256, 128))

    def damp_step(step, carry):
        e = step // 4
        chunk = step % 4
        wave = jnp.where(e == 0, wave_0, wave_1)
        degree = wave + ((iota((256, 128), 0) >> 2) & 1) + 2 * (iota((256, 128), 1) + 128 * chunk)
        degree = degree.astype(F32)
        term = degree * (degree + 1.0) * (IMPLICIT_FACTOR / (WAVES * (WAVES - 1)))
        stiffness = term * rate
        damp_ref[e, chunk] = stiffness / (1.0 + stiffness)
        return carry

    lax.fori_loop(0, 8, damp_step, 0)

    def flip_step(step, carry):
        i = step // TILES
        tile = step % TILES
        lanes = pl.ds(pl.multiple_of(256 * tile, 256), 256)
        flip_ref[i, lanes, :] = table_ref[i, :, lanes].T
        return carry

    lax.fori_loop(0, 2 * TILES, flip_step, 0)

    sent_1.wait_recv()

    rows_ref[...] = r1_ref[...].reshape(8 * NB, 128).astype(F32)
    for a in range(2):
        block = stack([rows_ref[pl.ds(4 * a + j, NB, stride=8), :] for j in range(4)]).T.astype(BF16)
        for t in range(8):
            s2_ref[2 * t + a] = block[16 * t : 16 * (t + 1)]
    r2_ref[lev] = s2_ref[lev]
    sent_2 = send_lev(s2_ref, r2_ref, 1)
    sent_2.wait_recv()

    data = r2_ref[...].reshape(256, 128)
    parity = (iota((256, 128), 0) >> 2) & 1
    side = iota((256, 128), 1) >> 6

    def chosen(q, e):
        return ((parity == q) & (side == e)).astype(F32).astype(BF16)

    jobs = [(e, step) for step in range(2) for e in range(2)]
    lefts = [jnp.concatenate([data * chosen(q, e) for q in range(2)], axis=1) for e in range(2)]
    spectral = [dot(lefts[e], leg_ref[:, 256 * step : 256 * (step + 1)]) for e, step in jobs]
    modal = [dot(mode1_ref[...], part.astype(BF16)) for part in spectral]
    for k, (e, step) in enumerate(jobs):
        damping = jnp.concatenate([damp_ref[e, 2 * step], damp_ref[e, 2 * step + 1]], axis=1)
        modal[k] = (modal[k] * damping).astype(BF16)
    for k, (e, step) in enumerate(jobs):
        solved = spectral[k] - dot(mode2_ref[...], modal[k])
        solved_ref[e, :, 256 * step : 256 * (step + 1)] = solved.astype(BF16)

    picked = []
    for e in range(2):
        back = dot_nt(solved_ref[e], leg_ref[...])
        picked.append(jnp.where(parity == 0, back[:, :128], back[:, 128:]))
    s3_ref[...] = jnp.where(side == 0, picked[0], picked[1]).astype(BF16).reshape(NL, 16, 128)
    r3_ref[lev] = s3_ref[lev]
    sent_3 = send_lev(s3_ref, r3_ref, 2)
    sent_3.wait_recv()

    for a in range(2):
        block = stack([r3_ref[2 * t + a] for t in range(8)]).astype(F32).T
        for j in range(4):
            rows_ref[pl.ds(4 * a + j, NB, stride=8), :] = block[NB * j : NB * (j + 1)]
    s4_ref[...] = rows_ref[...].astype(BF16).reshape(NB, 8, 128)
    r4_ref[blk] = s4_ref[blk]
    sent_4 = send_blk(s4_ref, r4_ref, 3)
    out_ref[:, :, :, pl.ds(LIVE, PSLOT - LIVE)] = jnp.zeros((2, 2, 4, PSLOT - LIVE), F32)
    sent_4.wait_recv()

    rows_ref[...] = r4_ref[...].reshape(8 * NB, 128).astype(F32)
    for i in range(2):
        four_ref[i] = stack([rows_ref[pl.ds(2 * a + i, NB, stride=8), :] for a in range(4)]).T

    for i in range(2):
        points = points_of(i)
        value = 0.0
        for group in range(2):
            left = []
            for tile in range(4 * group, 4 * group + 4):
                double = jnp.where(wave_ref[tile] == 0.0, 1.0, 2.0)
                real = four_ref[i, 16 * tile : 16 * tile + 8, :] * double
                imag = four_ref[i, 16 * tile + 8 : 16 * tile + 16, :] * double
                reals, imags = [], []
                for u in range(BLOCKS):
                    c = turn_ref[i, tile, 0, u]
                    s = turn_ref[i, tile, 1, u]
                    reals.append(real * c + imag * s)
                    imags.append(imag * c - real * s)
                left += [stack(reals).astype(BF16), stack(imags).astype(BF16)]
            right = flip_ref[i, 1024 * group : 1024 * (group + 1), :]
            value = value + dot(jnp.concatenate(left, axis=1), right)
        for u in range(BLOCKS):
            even = value[8 * u : 8 * u + 4]
            odd = value[8 * u + 4 : 8 * u + 8]
            live = iota((4, SPAN), 1) + SPAN * u < points
            out_ref[i, 0, :, SPAN * u : SPAN * (u + 1)] = jnp.where(live, even + odd, 0.0)
            out_ref[i, 1, :, SPAN * u : SPAN * (u + 1)] = jnp.where(live, even - odd, 0.0)

    for sent in (sent_1, sent_2, sent_3, sent_4):
        sent.wait_send()


def shards(grid_values, quad_weight, legendre, vertical_modes, eigenvalues, pair_latitude, wave_slot):
    vmem = pl.BlockSpec(memory_space=pltpu.VMEM)
    smem = pl.BlockSpec(memory_space=pltpu.SMEM)
    hbm = pl.BlockSpec(memory_space=pl.ANY)
    return pl.pallas_call(
        kernel,
        out_shape=pltpu.VMEM(grid_values.shape, F32),
        in_specs=[hbm, smem, hbm, vmem, vmem, smem, vmem, smem],
        out_specs=vmem,
        scratch_shapes=[
            pltpu.VMEM((2, 2, 4, PSLOT), F32),
            pltpu.VMEM((2, 2, 64, HALF), BF16),
            pltpu.VMEM((TILES, 8, 128), F32),
            pltpu.VMEM((2, 2, ROWS, SPAN), BF16),
            pltpu.VMEM((2, SPAN, 2 * WAVES), BF16),
            pltpu.VMEM((SPAN, 2 * WAVES), BF16),
            pltpu.VMEM((2, 2 * WAVES, SPAN), BF16),
            pltpu.VMEM((2, TILES, 2, BLOCKS, 8, 128), F32),
            pltpu.VMEM((2, 128, 128), F32),
            pltpu.VMEM((8 * NB, 128), F32),
            pltpu.VMEM((NB, 8, 128), BF16),
            pltpu.VMEM((NB, 8, 128), BF16),
            pltpu.VMEM((NL, 16, 128), BF16),
            pltpu.VMEM((NL, 16, 128), BF16),
            pltpu.VMEM((NL, 16, 128), BF16),
            pltpu.VMEM((NL, 16, 128), BF16),
            pltpu.VMEM((NB, 8, 128), BF16),
            pltpu.VMEM((NB, 8, 128), BF16),
            pltpu.VMEM((256, HALF), BF16),
            pltpu.VMEM((256, 256), BF16),
            pltpu.VMEM((256, 256), BF16),
            pltpu.VMEM((2, 4, 256, 128), F32),
            pltpu.VMEM((2, 256, HALF), BF16),
            pltpu.SemaphoreType.DMA((2,)),
            pltpu.SemaphoreType.DMA((4,)),
            pltpu.SemaphoreType.DMA((4,)),
        ],
        compiler_params=pltpu.CompilerParams(
            collective_id=0, has_side_effects=True, vmem_limit_bytes=60 * 1024 * 1024
        ),
        cost_estimate=pl.CostEstimate(flops=4_000_000_000, bytes_accessed=1_500_000, transcendentals=0),
    )(
        grid_values, quad_weight, legendre, vertical_modes, eigenvalues.reshape(1, LEVELS),
        pair_latitude, wave_slot.reshape(8, 128), wave_slot,
    )


def solution(mesh):
    in_specs = (
        P("blk", None, "lev", None),
        P("blk"),
        P("blk", None, None, None),
        P(),
        P(),
        P("blk"),
        P(),
    )
    out_specs = P("blk", None, "lev", None)
    return jax.shard_map(shards, mesh=mesh, in_specs=in_specs, out_specs=out_specs, check_vma=False)
```

```python
import jax
import jax.numpy as jnp
from jax import lax
from jax.experimental import pallas as pl
from jax.experimental.pallas import tpu as pltpu
from jax.sharding import PartitionSpec as P

MESH = pl.DeviceIdType.MESH
BF16 = jnp.bfloat16
F32 = jnp.float32

WAVES = 1024
HALF = 512
LEVELS = 64
NB = 32
NL = 16
SPAN = 256
BLOCKS = 22
ROWS = 8 * BLOCKS
TILES = WAVES // 128
LIVE = BLOCKS * SPAN
PSLOT = 6144
IMPLICIT_FACTOR = 4.0
PI = 3.141592653589793


def ring(step, size):
    return min(step, size - step)


BLK_PEERS = sorted(
    [(y, x) for y in range(8) for x in range(4) if (y, x) != (0, 0)],
    key=lambda d: (-ring(d[0], 8) - ring(d[1], 4), d),
)
LEV_PEERS = sorted(
    [(z, c) for z in range(8) for c in range(2) if (z, c) != (0, 0)],
    key=lambda d: (-ring(d[0], 8) - 0.5 * d[1], d),
)


def blk_peer(blk, peer):
    return (blk // 4 + peer[0]) % 8 * 4 + (blk % 4 + peer[1]) % 4


def lev_peer(lev, peer):
    return (lev // 2 + peer[0]) % 8 * 2 + (lev % 2 + peer[1]) % 2


def iota(shape, dim):
    return lax.broadcasted_iota(jnp.int32, shape, dim)


def dot(a, b):
    return jnp.dot(a, b, preferred_element_type=F32)


def dot_nt(a, b):
    return lax.dot_general(a, b, (((1,), (1,)), ((), ())), preferred_element_type=F32)


def dot_tn(a, b):
    return lax.dot_general(a, b, (((0,), (0,)), ((), ())), preferred_element_type=F32)


def split(x):
    high = x.astype(BF16)
    return high, (x - high.astype(F32)).astype(BF16)


def rotation(phase, points, inverse):
    turns = jnp.floor(phase * inverse + 0.5)
    x = (phase - turns * points) * inverse
    z = x * x
    sine = 0.0
    cosine = 0.0
    sin_terms = [PI]
    cos_terms = [1.0]
    for k in range(1, 7):
        sin_terms.append(-sin_terms[-1] * PI * PI / ((2 * k) * (2 * k + 1)))
        cos_terms.append(-cos_terms[-1] * PI * PI / ((2 * k - 1) * (2 * k)))
    sine = jnp.full_like(z, sin_terms[6])
    cosine = jnp.full_like(z, cos_terms[6])
    for k in range(5, -1, -1):
        sine = sine * z + sin_terms[k]
        cosine = cosine * z + cos_terms[k]
    sine = sine * x
    return 1.0 - 2.0 * sine * sine, -2.0 * sine * cosine


def turn(a, b):
    return a[0] * b[0] - a[1] * b[1], a[0] * b[1] + a[1] * b[0]


def stack(parts):
    return jnp.concatenate(parts, axis=0)


def kernel(
    grid_hbm, weight_hbm, legendre_hbm, modes_hbm, rates_hbm, cycle_hbm, slot_hbm, slots_hbm,
    out_ref,
    weight_ref, cycle_ref, slot_smem, slot_ref, modes_ref, rates_ref, grid_ref, raw_ref, wave_ref, x_ref, table_ref, rest_ref, flip_ref, turn_ref, four_ref,
    rows_ref, s1_ref, r1_ref, s2_ref, r2_ref, s3_ref, r3_ref, s4_ref, r4_ref,
    leg_ref, mode1_ref, mode2_ref, damp_ref, solved_ref,
    load_sem, send_sem, recv_sem,
):
    blk = lax.axis_index("blk")
    lev = lax.axis_index("lev")

    barrier = pltpu.get_barrier_semaphore()
    for peer in BLK_PEERS:
        pl.semaphore_signal(barrier, inc=1, device_id=(blk_peer(blk, peer), lev), device_id_type=MESH)
    for peer in LEV_PEERS:
        pl.semaphore_signal(barrier, inc=1, device_id=(blk, lev_peer(lev, peer)), device_id_type=MESH)

    small = [
        (slot_hbm, slot_ref), (cycle_hbm, cycle_ref), (weight_hbm, weight_ref),
        (slots_hbm, slot_smem), (modes_hbm, modes_ref), (rates_hbm, rates_ref),
    ]
    small_copies = [pltpu.make_async_copy(a, b, load_sem.at[2 + k]) for k, (a, b) in enumerate(small)]
    for copy in small_copies:
        copy.start()
    grid_copy = pltpu.make_async_copy(grid_hbm, grid_ref, load_sem.at[0])
    grid_copy.start()
    legendre_copy = pltpu.make_async_copy(
        legendre_hbm.at[pl.ds(2 * lev, 2)], raw_ref, load_sem.at[1]
    )
    legendre_copy.start()
    column = iota((128, WAVES), 1)
    pick = (iota((128, WAVES), 0) == 32 * (column & 3) + (column >> 5)).astype(F32).astype(BF16)
    for copy in small_copies[:3]:
        copy.wait()
    slots = slot_ref[...]
    halves = stack([slots >> 5, slots & 31]).astype(F32).astype(BF16)
    spread = dot(halves, pick)
    column = iota((8, WAVES), 1)
    mine = iota((8, WAVES), 0) == ((column & 31) >> 2)
    spread = jnp.where(mine, 32.0 * spread[:8] + spread[8:], 0.0)
    waves = jnp.sum(spread, axis=0, keepdims=True)
    for tile in range(TILES):
        wave_ref[tile] = jnp.broadcast_to(waves[:, 128 * tile : 128 * (tile + 1)], (8, 128))

    def points_of(i):
        return 20 + 4 * cycle_ref[i]

    def rotations(i, tile):
        points = jnp.full((8, 128), points_of(i), jnp.int32).astype(F32)
        inverse = 1.0 / points
        wave = wave_ref[tile]
        row = iota((8, 128), 0)
        place = row.astype(F32)
        extra = jnp.where(row == 0, 8.0, jnp.where(row == 1, 128.0, 2048.0))
        fine = rotation(place * wave, points, inverse)
        coarse = rotation(16.0 * place * wave, points, inverse)
        block = rotation(256.0 * place * wave, points, inverse)
        jump = rotation(extra * wave, points, inverse)

        def spread_row(pair, k):
            return tuple(jnp.broadcast_to(part[k : k + 1], (8, 128)) for part in pair)

        fine_next = turn(fine, spread_row(jump, 0))
        coarse_next = turn(coarse, spread_row(jump, 1))
        leap = spread_row(jump, 2)
        kept = (2.0 * wave < points).astype(F32)
        block = (block[0] * kept, block[1] * kept)
        block_1 = turn(block, leap)
        block_2 = turn(block_1, leap)

        high = [[], []]
        low = [[], []]
        for a in range(16):
            lead = spread_row(coarse if a < 8 else coarse_next, a % 8)
            first = turn(lead, fine)
            second = turn(lead, fine_next)
            for part in range(2):
                h, l = split(stack([first[part], second[part]]))
                high[part].append(h)
                low[part].append(l)
        table = jnp.concatenate([stack(high[0]), stack(high[1])], axis=1)
        rest = jnp.concatenate([stack(low[0]), stack(low[1])], axis=1)
        table_ref[i, :, pl.ds(pl.multiple_of(256 * tile, 256), 256)] = table
        turns = [spread_row((block, block_1, block_2)[u // 8], u % 8) for u in range(BLOCKS)]
        for u in range(BLOCKS):
            turn_ref[i, tile, 0, u], turn_ref[i, tile, 1, u] = turns[u]
        return table, rest, turns

    def transform(i, tile, table, rest, turns):
        x_high = x_ref[i, 0]
        sums = dot(
            jnp.concatenate([x_high, x_ref[i, 1], x_high], axis=1),
            jnp.concatenate([table, table, rest], axis=0),
        )
        real = jnp.zeros((8, 128), F32)
        imag = jnp.zeros((8, 128), F32)
        for u in range(BLOCKS):
            c, s = turns[u]
            p, q = sums[8 * u : 8 * u + 8, :128], sums[8 * u : 8 * u + 8, 128:]
            real = real + (c * p - s * q)
            imag = imag + (c * q + s * p)
        start = pl.multiple_of(16 * tile, 16)
        four_ref[i, pl.ds(start, 8), :] = real
        four_ref[i, pl.ds(start + 8, 8), :] = imag

    def early_step(tile, carry):
        _, rest, _ = rotations(0, tile)
        rest_ref[:, pl.ds(pl.multiple_of(256 * tile, 256), 256)] = rest
        return carry

    lax.fori_loop(0, 8, early_step, 0, unroll=8)

    grid_copy.wait()

    def fold_step(step, carry):
        i = step // (BLOCKS // 2)
        k = step % (BLOCKS // 2)
        points = points_of(i)
        scale = jnp.full((4, SPAN), weight_ref[i], F32) / jnp.full((4, SPAN), points, jnp.int32).astype(F32)
        rows = []
        for half in range(2):
            start = pl.multiple_of(512 * k + 256 * half, 256)
            live = iota((4, SPAN), 1) + start < points
            north = grid_ref[i, 0, :, pl.ds(start, SPAN)]
            south = grid_ref[i, 1, :, pl.ds(start, SPAN)]
            rows.append(jnp.where(live, (north + south) * scale, 0.0))
            rows.append(jnp.where(live, (north - south) * scale, 0.0))
        high, low = split(stack(rows))
        x_ref[i, 0, pl.ds(pl.multiple_of(16 * k, 16), 16), :] = high
        x_ref[i, 1, pl.ds(pl.multiple_of(16 * k, 16), 16), :] = low
        return carry

    lax.fori_loop(0, BLOCKS, fold_step, 0, unroll=2)

    def early_transform(tile, carry):
        lanes = pl.ds(pl.multiple_of(256 * tile, 256), 256)
        turns = [(turn_ref[0, tile, 0, u], turn_ref[0, tile, 1, u]) for u in range(BLOCKS)]
        transform(0, tile, table_ref[0, :, lanes], rest_ref[:, lanes], turns)
        return carry

    def analyse_step(step, carry):
        transform(step // TILES, step % TILES, *rotations(step // TILES, step % TILES))
        return carry

    lax.fori_loop(0, 8, early_transform, 0, unroll=8)
    lax.fori_loop(8, 2 * TILES, analyse_step, 0, unroll=8)

    for i in range(2):
        flipped = four_ref[i].T
        for a in range(4):
            rows_ref[pl.ds(2 * a + i, NB, stride=8), :] = flipped[NB * a : NB * (a + 1)]
    s1_ref[...] = rows_ref[...].astype(BF16).reshape(NB, 8, 128)
    r1_ref[blk] = s1_ref[blk]
    pl.semaphore_wait(barrier, NB + NL - 2)

    def send_blk(source, target, sem):
        for peer in BLK_PEERS:
            other = blk_peer(blk, peer)
            pltpu.make_async_remote_copy(
                src_ref=source.at[other],
                dst_ref=target.at[blk],
                send_sem=send_sem.at[sem],
                recv_sem=recv_sem.at[sem],
                device_id=(other, lev),
                device_id_type=MESH,
            ).start()
        rows = pl.ds(0, NB - 1)
        return pltpu.make_async_remote_copy(
            src_ref=source.at[rows], dst_ref=target.at[rows],
            send_sem=send_sem.at[sem], recv_sem=recv_sem.at[sem],
            device_id=(blk_peer(blk, BLK_PEERS[0]), lev), device_id_type=MESH,
        )

    def send_lev(source, target, sem):
        for peer in LEV_PEERS:
            other = lev_peer(lev, peer)
            pltpu.make_async_remote_copy(
                src_ref=source.at[other],
                dst_ref=target.at[lev],
                send_sem=send_sem.at[sem],
                recv_sem=recv_sem.at[sem],
                device_id=(blk, other),
                device_id_type=MESH,
            ).start()
        rows = pl.ds(0, NL - 1)
        return pltpu.make_async_remote_copy(
            src_ref=source.at[rows], dst_ref=target.at[rows],
            send_sem=send_sem.at[sem], recv_sem=recv_sem.at[sem],
            device_id=(blk, lev_peer(lev, LEV_PEERS[0])), device_id_type=MESH,
        )

    sent_1 = send_blk(s1_ref, r1_ref, 0)

    legendre_copy.wait()
    for copy in small_copies[3:]:
        copy.wait()
    wave_0 = slot_smem[32 * blk + 2 * lev]
    wave_1 = slot_smem[32 * blk + 2 * lev + 1]
    row = iota((256, 256), 0)
    source = ((row >> 6) & 1) * 128 + (row >> 7) * 64 + 2 * (row & 31) + ((row >> 5) & 1)
    reorder = (iota((256, 256), 1) == source).astype(F32).astype(BF16)
    ordered = dot(reorder, raw_ref[...].reshape(256, HALF))
    row = iota((256, HALF), 0)
    degree = jnp.where(((row >> 6) & 1) == 0, wave_0, wave_1) + (row >> 7) + 2 * iota((256, HALF), 1)
    leg_ref[...] = jnp.where(degree <= WAVES - 1, ordered, 0.0).astype(BF16)

    def spread_rows(shape, row_dim):
        row = iota(shape, row_dim)
        return iota(shape, 1 - row_dim) == 4 * (row >> 4) + (row & 3)

    tall = spread_rows((256, LEVELS), 0).astype(F32).astype(BF16)
    wide = spread_rows((LEVELS, 256), 1).astype(F32).astype(BF16)
    same = ((iota((256, 256), 0) >> 2) & 3) == ((iota((256, 256), 1) >> 2) & 3)
    for part, modes in enumerate(split(modes_ref[...])):
        full = dot(tall, dot(modes, wide).astype(BF16))
        mode2_ref[256 * part : 256 * (part + 1), :] = jnp.where(same, full, 0.0).astype(BF16)
        full = dot(tall, dot_tn(modes, wide).astype(BF16))
        mode1_ref[256 * part : 256 * (part + 1), :] = jnp.where(same, full, 0.0).astype(BF16)

    rate = jnp.sum(
        jnp.where(spread_rows((256, LEVELS), 0), jnp.broadcast_to(rates_ref[...], (256, LEVELS)), 0.0),
        axis=1, keepdims=True,
    )
    rate = jnp.broadcast_to(rate, (256, 128))

    def damp_step(step, carry):
        e = step // 4
        chunk = step % 4
        wave = jnp.where(e == 0, wave_0, wave_1)
        degree = wave + ((iota((256, 128), 0) >> 2) & 1) + 2 * (iota((256, 128), 1) + 128 * chunk)
        degree = degree.astype(F32)
        term = degree * (degree + 1.0) * (IMPLICIT_FACTOR / (WAVES * (WAVES - 1)))
        stiffness = term * rate
        damp_ref[e, chunk] = stiffness / (1.0 + stiffness)
        return carry

    lax.fori_loop(0, 8, damp_step, 0)

    def flip_step(step, carry):
        i = step // TILES
        tile = step % TILES
        lanes = pl.ds(pl.multiple_of(256 * tile, 256), 256)
        flip_ref[i, lanes, :] = table_ref[i, :, lanes].T
        return carry

    lax.fori_loop(0, 2 * TILES, flip_step, 0)

    sent_1.wait_recv()

    rows_ref[...] = r1_ref[...].reshape(8 * NB, 128).astype(F32)
    for a in range(2):
        block = stack([rows_ref[pl.ds(4 * a + j, NB, stride=8), :] for j in range(4)]).T.astype(BF16)
        for t in range(8):
            s2_ref[2 * t + a] = block[16 * t : 16 * (t + 1)]
    r2_ref[lev] = s2_ref[lev]
    sent_2 = send_lev(s2_ref, r2_ref, 1)
    sent_2.wait_recv()

    data = r2_ref[...].reshape(256, 128)
    parity = (iota((256, 128), 0) >> 2) & 1
    side = iota((256, 128), 1) >> 6

    def chosen(q, e):
        return ((parity == q) & (side == e)).astype(F32).astype(BF16)

    jobs = [(e, step) for step in range(2) for e in range(2)]
    lefts = [jnp.concatenate([data * chosen(q, e) for q in range(2)], axis=1) for e in range(2)]
    spectral = [dot(lefts[e], leg_ref[:, 256 * step : 256 * (step + 1)]) for e, step in jobs]
    modal = [dot(mode1_ref[...], part.astype(BF16)) for part in spectral]
    modal = [part[:256] + part[256:] for part in modal]
    for k, (e, step) in enumerate(jobs):
        damping = jnp.concatenate([damp_ref[e, 2 * step], damp_ref[e, 2 * step + 1]], axis=1)
        modal[k] = (modal[k] * damping).astype(BF16)
    for k, (e, step) in enumerate(jobs):
        change = dot(mode2_ref[...], modal[k])
        solved = spectral[k] - (change[:256] + change[256:])
        solved_ref[e, :, 256 * step : 256 * (step + 1)] = solved.astype(BF16)

    picked = []
    for e in range(2):
        back = dot_nt(solved_ref[e], leg_ref[...])
        picked.append(jnp.where(parity == 0, back[:, :128], back[:, 128:]))
    s3_ref[...] = jnp.where(side == 0, picked[0], picked[1]).astype(BF16).reshape(NL, 16, 128)
    r3_ref[lev] = s3_ref[lev]
    sent_3 = send_lev(s3_ref, r3_ref, 2)
    sent_3.wait_recv()

    for a in range(2):
        block = stack([r3_ref[2 * t + a] for t in range(8)]).astype(F32).T
        for j in range(4):
            rows_ref[pl.ds(4 * a + j, NB, stride=8), :] = block[NB * j : NB * (j + 1)]
    s4_ref[...] = rows_ref[...].astype(BF16).reshape(NB, 8, 128)
    r4_ref[blk] = s4_ref[blk]
    sent_4 = send_blk(s4_ref, r4_ref, 3)
    out_ref[:, :, :, pl.ds(LIVE, PSLOT - LIVE)] = jnp.zeros((2, 2, 4, PSLOT - LIVE), F32)
    sent_4.wait_recv()

    rows_ref[...] = r4_ref[...].reshape(8 * NB, 128).astype(F32)
    for i in range(2):
        four_ref[i] = stack([rows_ref[pl.ds(2 * a + i, NB, stride=8), :] for a in range(4)]).T

    for i in range(2):
        points = points_of(i)
        value = 0.0
        for group in range(2):
            left = []
            for tile in range(4 * group, 4 * group + 4):
                double = jnp.where(wave_ref[tile] == 0.0, 1.0, 2.0)
                real = four_ref[i, 16 * tile : 16 * tile + 8, :] * double
                imag = four_ref[i, 16 * tile + 8 : 16 * tile + 16, :] * double
                reals, imags = [], []
                for u in range(BLOCKS):
                    c = turn_ref[i, tile, 0, u]
                    s = turn_ref[i, tile, 1, u]
                    reals.append(real * c + imag * s)
                    imags.append(imag * c - real * s)
                left += [stack(reals).astype(BF16), stack(imags).astype(BF16)]
            right = flip_ref[i, 1024 * group : 1024 * (group + 1), :]
            value = value + dot(jnp.concatenate(left, axis=1), right)
        for u in range(BLOCKS):
            even = value[8 * u : 8 * u + 4]
            odd = value[8 * u + 4 : 8 * u + 8]
            live = iota((4, SPAN), 1) + SPAN * u < points
            out_ref[i, 0, :, SPAN * u : SPAN * (u + 1)] = jnp.where(live, even + odd, 0.0)
            out_ref[i, 1, :, SPAN * u : SPAN * (u + 1)] = jnp.where(live, even - odd, 0.0)

    for sent in (sent_1, sent_2, sent_3, sent_4):
        sent.wait_send()


def shards(grid_values, quad_weight, legendre, vertical_modes, eigenvalues, pair_latitude, wave_slot):
    vmem = pl.BlockSpec(memory_space=pltpu.VMEM)
    hbm = pl.BlockSpec(memory_space=pl.ANY)
    return pl.pallas_call(
        kernel,
        out_shape=pltpu.VMEM(grid_values.shape, F32),
        in_specs=[hbm] * 8,
        out_specs=vmem,
        scratch_shapes=[
            pltpu.SMEM((2,), F32),
            pltpu.SMEM((2,), jnp.int32),
            pltpu.SMEM((WAVES,), jnp.int32),
            pltpu.VMEM((8, 128), jnp.int32),
            pltpu.VMEM((LEVELS, LEVELS), F32),
            pltpu.VMEM((1, LEVELS), F32),
            pltpu.VMEM((2, 2, 4, PSLOT), F32),
            pltpu.VMEM((2, 2, 64, HALF), BF16),
            pltpu.VMEM((TILES, 8, 128), F32),
            pltpu.VMEM((2, 2, ROWS, SPAN), BF16),
            pltpu.VMEM((2, SPAN, 2 * WAVES), BF16),
            pltpu.VMEM((SPAN, 2 * WAVES), BF16),
            pltpu.VMEM((2, 2 * WAVES, SPAN), BF16),
            pltpu.VMEM((2, TILES, 2, BLOCKS, 8, 128), F32),
            pltpu.VMEM((2, 128, 128), F32),
            pltpu.VMEM((8 * NB, 128), F32),
            pltpu.VMEM((NB, 8, 128), BF16),
            pltpu.VMEM((NB, 8, 128), BF16),
            pltpu.VMEM((NL, 16, 128), BF16),
            pltpu.VMEM((NL, 16, 128), BF16),
            pltpu.VMEM((NL, 16, 128), BF16),
            pltpu.VMEM((NL, 16, 128), BF16),
            pltpu.VMEM((NB, 8, 128), BF16),
            pltpu.VMEM((NB, 8, 128), BF16),
            pltpu.VMEM((256, HALF), BF16),
            pltpu.VMEM((512, 256), BF16),
            pltpu.VMEM((512, 256), BF16),
            pltpu.VMEM((2, 4, 256, 128), F32),
            pltpu.VMEM((2, 256, HALF), BF16),
            pltpu.SemaphoreType.DMA((8,)),
            pltpu.SemaphoreType.DMA((4,)),
            pltpu.SemaphoreType.DMA((4,)),
        ],
        compiler_params=pltpu.CompilerParams(
            collective_id=0, has_side_effects=True, vmem_limit_bytes=60 * 1024 * 1024
        ),
        cost_estimate=pl.CostEstimate(flops=4_000_000_000, bytes_accessed=1_500_000, transcendentals=0),
    )(
        grid_values, quad_weight, legendre, vertical_modes, eigenvalues.reshape(1, LEVELS),
        pair_latitude, wave_slot.reshape(8, 128), wave_slot,
    )


def solution(mesh):
    in_specs = (
        P("blk", None, "lev", None),
        P("blk"),
        P("blk", None, None, None),
        P(),
        P(),
        P("blk"),
        P(),
    )
    out_specs = P("blk", None, "lev", None)
    return jax.shard_map(shards, mesh=mesh, in_specs=in_specs, out_specs=out_specs, check_vma=False)
```

```python
import jax
import jax.numpy as jnp
from jax import lax
from jax.experimental import pallas as pl
from jax.experimental.pallas import tpu as pltpu
from jax.sharding import PartitionSpec as P

MESH = pl.DeviceIdType.MESH
BF16 = jnp.bfloat16
F32 = jnp.float32

WAVES = 1024
HALF = 512
LEVELS = 64
NB = 32
NL = 16
SPAN = 256
BLOCKS = 22
ROWS = 8 * BLOCKS
TILES = WAVES // 128
LIVE = BLOCKS * SPAN
PSLOT = 6144
IMPLICIT_FACTOR = 4.0
PI = 3.141592653589793


def ring(step, size):
    return min(step, size - step)


BLK_PEERS = sorted(
    [(y, x) for y in range(8) for x in range(4) if (y, x) != (0, 0)],
    key=lambda d: (-ring(d[0], 8) - ring(d[1], 4), d),
)
LEV_PEERS = sorted(
    [(z, c) for z in range(8) for c in range(2) if (z, c) != (0, 0)],
    key=lambda d: (-ring(d[0], 8) - 0.5 * d[1], d),
)


def blk_peer(blk, peer):
    return (blk // 4 + peer[0]) % 8 * 4 + (blk % 4 + peer[1]) % 4


def lev_peer(lev, peer):
    return (lev // 2 + peer[0]) % 8 * 2 + (lev % 2 + peer[1]) % 2


def iota(shape, dim):
    return lax.broadcasted_iota(jnp.int32, shape, dim)


def dot(a, b):
    return jnp.dot(a, b, preferred_element_type=F32)


def dot_nt(a, b):
    return lax.dot_general(a, b, (((1,), (1,)), ((), ())), preferred_element_type=F32)


def dot_tn(a, b):
    return lax.dot_general(a, b, (((0,), (0,)), ((), ())), preferred_element_type=F32)


def split(x):
    high = x.astype(BF16)
    return high, (x - high.astype(F32)).astype(BF16)


def rotation(phase, points, inverse):
    turns = jnp.floor(phase * inverse + 0.5)
    x = (phase - turns * points) * inverse
    z = x * x
    sine = 0.0
    cosine = 0.0
    sin_terms = [PI]
    cos_terms = [1.0]
    for k in range(1, 7):
        sin_terms.append(-sin_terms[-1] * PI * PI / ((2 * k) * (2 * k + 1)))
        cos_terms.append(-cos_terms[-1] * PI * PI / ((2 * k - 1) * (2 * k)))
    sine = jnp.full_like(z, sin_terms[6])
    cosine = jnp.full_like(z, cos_terms[6])
    for k in range(5, -1, -1):
        sine = sine * z + sin_terms[k]
        cosine = cosine * z + cos_terms[k]
    sine = sine * x
    return 1.0 - 2.0 * sine * sine, -2.0 * sine * cosine


def turn(a, b):
    return a[0] * b[0] - a[1] * b[1], a[0] * b[1] + a[1] * b[0]


def stack(parts):
    return jnp.concatenate(parts, axis=0)


def kernel(
    grid_hbm, weight_hbm, legendre_hbm, modes_hbm, rates_hbm, cycle_hbm, slot_hbm, slots_hbm,
    out_ref,
    weight_ref, cycle_ref, slot_smem, slot_ref, modes_ref, rates_ref, grid_ref, raw_ref, wave_ref, x_ref, table_ref, rest_ref, flip_ref, turn_ref, four_ref,
    rows_ref, s1_ref, r1_ref, s2_ref, r2_ref, s3_ref, r3_ref, s4_ref, r4_ref,
    leg_ref, mode1_ref, mode2_ref, damp_ref, solved_ref,
    load_sem, send_sem, recv_sem,
):
    blk = lax.axis_index("blk")
    lev = lax.axis_index("lev")

    barrier = pltpu.get_barrier_semaphore()
    greetings = [(ring(y, 8) + ring(x, 4), "blk", (y, x)) for y, x in BLK_PEERS]
    greetings += [(ring(z, 8) + 0.75 * c, "lev", (z, c)) for z, c in LEV_PEERS]
    for _, axis, peer in sorted(greetings, reverse=True):
        target = (blk_peer(blk, peer), lev) if axis == "blk" else (blk, lev_peer(lev, peer))
        pl.semaphore_signal(barrier, inc=1, device_id=target, device_id_type=MESH)
    small = [
        (slot_hbm, slot_ref), (cycle_hbm, cycle_ref), (weight_hbm, weight_ref),
        (slots_hbm, slot_smem), (modes_hbm, modes_ref), (rates_hbm, rates_ref),
    ]
    small_copies = [pltpu.make_async_copy(a, b, load_sem.at[2 + k]) for k, (a, b) in enumerate(small)]
    for copy in small_copies:
        copy.start()
    grid_copy = pltpu.make_async_copy(grid_hbm, grid_ref, load_sem.at[0])
    grid_copy.start()
    legendre_copy = pltpu.make_async_copy(
        legendre_hbm.at[pl.ds(2 * lev, 2)], raw_ref, load_sem.at[1]
    )
    legendre_copy.start()
    column = iota((128, WAVES), 1)
    pick = (iota((128, WAVES), 0) == 32 * (column & 3) + (column >> 5)).astype(F32).astype(BF16)
    for copy in small_copies[:3]:
        copy.wait()
    slots = slot_ref[...]
    halves = stack([slots >> 5, slots & 31]).astype(F32).astype(BF16)
    spread = dot(halves, pick)
    column = iota((8, WAVES), 1)
    mine = iota((8, WAVES), 0) == ((column & 31) >> 2)
    spread = jnp.where(mine, 32.0 * spread[:8] + spread[8:], 0.0)
    waves = jnp.sum(spread, axis=0, keepdims=True)
    for tile in range(TILES):
        wave_ref[tile] = jnp.broadcast_to(waves[:, 128 * tile : 128 * (tile + 1)], (8, 128))

    def points_of(i):
        return 20 + 4 * cycle_ref[i]

    def rotations(i, tile):
        points = jnp.full((8, 128), points_of(i), jnp.int32).astype(F32)
        inverse = 1.0 / points
        wave = wave_ref[tile]
        row = iota((8, 128), 0)
        place = row.astype(F32)
        extra = jnp.where(row == 0, 8.0, jnp.where(row == 1, 128.0, 2048.0))
        fine = rotation(place * wave, points, inverse)
        coarse = rotation(16.0 * place * wave, points, inverse)
        block = rotation(256.0 * place * wave, points, inverse)
        jump = rotation(extra * wave, points, inverse)

        def spread_row(pair, k):
            return tuple(jnp.broadcast_to(part[k : k + 1], (8, 128)) for part in pair)

        fine_next = turn(fine, spread_row(jump, 0))
        coarse_next = turn(coarse, spread_row(jump, 1))
        leap = spread_row(jump, 2)
        kept = (2.0 * wave < points).astype(F32)
        block = (block[0] * kept, block[1] * kept)
        block_1 = turn(block, leap)
        block_2 = turn(block_1, leap)

        high = [[], []]
        low = [[], []]
        for a in range(16):
            lead = spread_row(coarse if a < 8 else coarse_next, a % 8)
            first = turn(lead, fine)
            second = turn(lead, fine_next)
            for part in range(2):
                h, l = split(stack([first[part], second[part]]))
                high[part].append(h)
                low[part].append(l)
        table = jnp.concatenate([stack(high[0]), stack(high[1])], axis=1)
        rest = jnp.concatenate([stack(low[0]), stack(low[1])], axis=1)
        table_ref[i, :, pl.ds(pl.multiple_of(256 * tile, 256), 256)] = table
        turns = [spread_row((block, block_1, block_2)[u // 8], u % 8) for u in range(BLOCKS)]
        for u in range(BLOCKS):
            turn_ref[i, tile, 0, u], turn_ref[i, tile, 1, u] = turns[u]
        return table, rest, turns

    def transform(i, tile, table, rest, turns):
        x_high = x_ref[i, 0]
        sums = dot(
            jnp.concatenate([x_high, x_ref[i, 1], x_high], axis=1),
            jnp.concatenate([table, table, rest], axis=0),
        )
        real = jnp.zeros((8, 128), F32)
        imag = jnp.zeros((8, 128), F32)
        for u in range(BLOCKS):
            c, s = turns[u]
            p, q = sums[8 * u : 8 * u + 8, :128], sums[8 * u : 8 * u + 8, 128:]
            real = real + (c * p - s * q)
            imag = imag + (c * q + s * p)
        start = pl.multiple_of(16 * tile, 16)
        four_ref[i, pl.ds(start, 8), :] = real
        four_ref[i, pl.ds(start + 8, 8), :] = imag

    def early_step(tile, carry):
        _, rest, _ = rotations(0, tile)
        rest_ref[:, pl.ds(pl.multiple_of(256 * tile, 256), 256)] = rest
        return carry

    lax.fori_loop(0, 8, early_step, 0, unroll=8)

    grid_copy.wait()

    def fold_step(step, carry):
        i = step // (BLOCKS // 2)
        k = step % (BLOCKS // 2)
        points = points_of(i)
        scale = jnp.full((4, SPAN), weight_ref[i], F32) / jnp.full((4, SPAN), points, jnp.int32).astype(F32)
        rows = []
        for half in range(2):
            start = pl.multiple_of(512 * k + 256 * half, 256)
            live = iota((4, SPAN), 1) + start < points
            north = grid_ref[i, 0, :, pl.ds(start, SPAN)]
            south = grid_ref[i, 1, :, pl.ds(start, SPAN)]
            rows.append(jnp.where(live, (north + south) * scale, 0.0))
            rows.append(jnp.where(live, (north - south) * scale, 0.0))
        high, low = split(stack(rows))
        x_ref[i, 0, pl.ds(pl.multiple_of(16 * k, 16), 16), :] = high
        x_ref[i, 1, pl.ds(pl.multiple_of(16 * k, 16), 16), :] = low
        return carry

    lax.fori_loop(0, BLOCKS, fold_step, 0, unroll=2)

    def early_transform(tile, carry):
        lanes = pl.ds(pl.multiple_of(256 * tile, 256), 256)
        turns = [(turn_ref[0, tile, 0, u], turn_ref[0, tile, 1, u]) for u in range(BLOCKS)]
        transform(0, tile, table_ref[0, :, lanes], rest_ref[:, lanes], turns)
        return carry

    def analyse_step(step, carry):
        transform(step // TILES, step % TILES, *rotations(step // TILES, step % TILES))
        return carry

    lax.fori_loop(0, 8, early_transform, 0, unroll=8)
    lax.fori_loop(8, 2 * TILES, analyse_step, 0, unroll=8)

    for i in range(2):
        flipped = four_ref[i].T
        for a in range(4):
            rows_ref[pl.ds(2 * a + i, NB, stride=8), :] = flipped[NB * a : NB * (a + 1)]
    s1_ref[...] = rows_ref[...].astype(BF16).reshape(NB, 8, 128)
    r1_ref[blk] = s1_ref[blk]
    pl.semaphore_wait(barrier, NB + NL - 2)

    def send_blk(source, target, sem):
        for peer in BLK_PEERS:
            other = blk_peer(blk, peer)
            pltpu.make_async_remote_copy(
                src_ref=source.at[other],
                dst_ref=target.at[blk],
                send_sem=send_sem.at[sem],
                recv_sem=recv_sem.at[sem],
                device_id=(other, lev),
                device_id_type=MESH,
            ).start()
        rows = pl.ds(0, NB - 1)
        return pltpu.make_async_remote_copy(
            src_ref=source.at[rows], dst_ref=target.at[rows],
            send_sem=send_sem.at[sem], recv_sem=recv_sem.at[sem],
            device_id=(blk_peer(blk, BLK_PEERS[0]), lev), device_id_type=MESH,
        )

    def send_lev(source, target, sem, core=None):
        def start(other):
            pltpu.make_async_remote_copy(
                src_ref=source.at[other],
                dst_ref=target.at[lev],
                send_sem=send_sem.at[sem],
                recv_sem=recv_sem.at[sem],
                device_id=(blk, other),
                device_id_type=MESH,
            ).start()

        if core is None:
            for peer in LEV_PEERS:
                start(lev_peer(lev, peer))
        else:
            for step in sorted(range(1, 8), key=lambda z: -ring(z, 8)):
                start((lev // 2 + step) % 8 * 2 + core)
            pl.when(lev % 2 != core)(lambda: start(lev // 2 * 2 + core))
        rows = pl.ds(0, NL - 1)
        return pltpu.make_async_remote_copy(
            src_ref=source.at[rows], dst_ref=target.at[rows],
            send_sem=send_sem.at[sem], recv_sem=recv_sem.at[sem],
            device_id=(blk, lev_peer(lev, LEV_PEERS[0])), device_id_type=MESH,
        )

    sent_1 = send_blk(s1_ref, r1_ref, 0)

    legendre_copy.wait()
    for copy in small_copies[3:]:
        copy.wait()
    wave_0 = slot_smem[32 * blk + 2 * lev]
    wave_1 = slot_smem[32 * blk + 2 * lev + 1]
    row = iota((256, 256), 0)
    source = ((row >> 6) & 1) * 128 + (row >> 7) * 64 + 2 * (row & 31) + ((row >> 5) & 1)
    reorder = (iota((256, 256), 1) == source).astype(F32).astype(BF16)
    ordered = dot(reorder, raw_ref[...].reshape(256, HALF))
    row = iota((256, HALF), 0)
    degree = jnp.where(((row >> 6) & 1) == 0, wave_0, wave_1) + (row >> 7) + 2 * iota((256, HALF), 1)
    leg_ref[...] = jnp.where(degree <= WAVES - 1, ordered, 0.0).astype(BF16)

    def spread_rows(shape, row_dim):
        row = iota(shape, row_dim)
        return iota(shape, 1 - row_dim) == 4 * (row >> 4) + (row & 3)

    tall = spread_rows((256, LEVELS), 0).astype(F32).astype(BF16)
    wide = spread_rows((LEVELS, 256), 1).astype(F32).astype(BF16)
    same = ((iota((256, 256), 0) >> 2) & 3) == ((iota((256, 256), 1) >> 2) & 3)
    for part, modes in enumerate(split(modes_ref[...])):
        full = dot(tall, dot(modes, wide).astype(BF16))
        mode2_ref[256 * part : 256 * (part + 1), :] = jnp.where(same, full, 0.0).astype(BF16)
        full = dot(tall, dot_tn(modes, wide).astype(BF16))
        mode1_ref[256 * part : 256 * (part + 1), :] = jnp.where(same, full, 0.0).astype(BF16)

    rate = jnp.sum(
        jnp.where(spread_rows((256, LEVELS), 0), jnp.broadcast_to(rates_ref[...], (256, LEVELS)), 0.0),
        axis=1, keepdims=True,
    )
    rate = jnp.broadcast_to(rate, (256, 128))

    def damp_step(step, carry):
        e = step // 4
        chunk = step % 4
        wave = jnp.where(e == 0, wave_0, wave_1)
        degree = wave + ((iota((256, 128), 0) >> 2) & 1) + 2 * (iota((256, 128), 1) + 128 * chunk)
        degree = degree.astype(F32)
        term = degree * (degree + 1.0) * (IMPLICIT_FACTOR / (WAVES * (WAVES - 1)))
        stiffness = term * rate
        damp_ref[e, chunk] = stiffness / (1.0 + stiffness)
        return carry

    lax.fori_loop(0, 8, damp_step, 0)

    def flip_step(step, carry):
        i = step // TILES
        tile = step % TILES
        lanes = pl.ds(pl.multiple_of(256 * tile, 256), 256)
        flip_ref[i, lanes, :] = table_ref[i, :, lanes].T
        return carry

    lax.fori_loop(0, 2 * TILES, flip_step, 0)

    sent_1.wait_recv()

    rows_ref[...] = r1_ref[...].reshape(8 * NB, 128).astype(F32)
    for a in range(2):
        block = stack([rows_ref[pl.ds(4 * a + j, NB, stride=8), :] for j in range(4)]).T.astype(BF16)
        for t in range(8):
            s2_ref[2 * t + a] = block[16 * t : 16 * (t + 1)]
        sent_2 = send_lev(s2_ref, r2_ref, 1, a)
    r2_ref[lev] = s2_ref[lev]
    parity = (iota((256, 128), 0) >> 2) & 1
    side = iota((256, 128), 1) >> 6

    def chosen(q, e):
        return ((parity == q) & (side == e)).astype(F32).astype(BF16)

    sent_2.wait_recv()

    data = r2_ref[...].reshape(256, 128)
    jobs = [(e, step) for step in range(2) for e in range(2)]
    lefts = [jnp.concatenate([data * chosen(q, e) for q in range(2)], axis=1) for e in range(2)]
    spectral = [dot(lefts[e], leg_ref[:, 256 * step : 256 * (step + 1)]) for e, step in jobs]
    modal = [dot(mode1_ref[...], part.astype(BF16)) for part in spectral]
    modal = [part[:256] + part[256:] for part in modal]
    for k, (e, step) in enumerate(jobs):
        damping = jnp.concatenate([damp_ref[e, 2 * step], damp_ref[e, 2 * step + 1]], axis=1)
        modal[k] = (modal[k] * damping).astype(BF16)
    for k, (e, step) in enumerate(jobs):
        change = dot(mode2_ref[...], modal[k])
        solved = spectral[k] - (change[:256] + change[256:])
        solved_ref[e, :, 256 * step : 256 * (step + 1)] = solved.astype(BF16)

    picked = []
    for e in range(2):
        back = dot_nt(solved_ref[e], leg_ref[...])
        picked.append(jnp.where(parity == 0, back[:, :128], back[:, 128:]))
    s3_ref[...] = jnp.where(side == 0, picked[0], picked[1]).astype(BF16).reshape(NL, 16, 128)
    sent_3 = send_lev(s3_ref, r3_ref, 2)
    r3_ref[lev] = s3_ref[lev]
    sent_3.wait_recv()

    for a in range(2):
        block = stack([r3_ref[2 * t + a] for t in range(8)]).astype(F32).T
        for j in range(4):
            rows_ref[pl.ds(4 * a + j, NB, stride=8), :] = block[NB * j : NB * (j + 1)]
    s4_ref[...] = rows_ref[...].astype(BF16).reshape(NB, 8, 128)
    sent_4 = send_blk(s4_ref, r4_ref, 3)
    r4_ref[blk] = s4_ref[blk]
    out_ref[:, :, :, pl.ds(LIVE, PSLOT - LIVE)] = jnp.zeros((2, 2, 4, PSLOT - LIVE), F32)
    sent_4.wait_recv()

    rows_ref[...] = r4_ref[...].reshape(8 * NB, 128).astype(F32)
    for i in range(2):
        four_ref[i] = stack([rows_ref[pl.ds(2 * a + i, NB, stride=8), :] for a in range(4)]).T

    for i in range(2):
        points = points_of(i)
        value = 0.0
        for group in range(2):
            left = []
            for tile in range(4 * group, 4 * group + 4):
                double = jnp.where(wave_ref[tile] == 0.0, 1.0, 2.0)
                real = four_ref[i, 16 * tile : 16 * tile + 8, :] * double
                imag = four_ref[i, 16 * tile + 8 : 16 * tile + 16, :] * double
                reals, imags = [], []
                for u in range(BLOCKS):
                    c = turn_ref[i, tile, 0, u]
                    s = turn_ref[i, tile, 1, u]
                    reals.append(real * c + imag * s)
                    imags.append(imag * c - real * s)
                left += [stack(reals).astype(BF16), stack(imags).astype(BF16)]
            right = flip_ref[i, 1024 * group : 1024 * (group + 1), :]
            value = value + dot(jnp.concatenate(left, axis=1), right)
        for u in range(BLOCKS):
            even = value[8 * u : 8 * u + 4]
            odd = value[8 * u + 4 : 8 * u + 8]
            live = iota((4, SPAN), 1) + SPAN * u < points
            out_ref[i, 0, :, SPAN * u : SPAN * (u + 1)] = jnp.where(live, even + odd, 0.0)
            out_ref[i, 1, :, SPAN * u : SPAN * (u + 1)] = jnp.where(live, even - odd, 0.0)

    for sent in (sent_1, sent_2, sent_3, sent_4):
        sent.wait_send()


def shards(grid_values, quad_weight, legendre, vertical_modes, eigenvalues, pair_latitude, wave_slot):
    vmem = pl.BlockSpec(memory_space=pltpu.VMEM)
    hbm = pl.BlockSpec(memory_space=pl.ANY)
    return pl.pallas_call(
        kernel,
        out_shape=pltpu.VMEM(grid_values.shape, F32),
        in_specs=[hbm] * 8,
        out_specs=vmem,
        scratch_shapes=[
            pltpu.SMEM((2,), F32),
            pltpu.SMEM((2,), jnp.int32),
            pltpu.SMEM((WAVES,), jnp.int32),
            pltpu.VMEM((8, 128), jnp.int32),
            pltpu.VMEM((LEVELS, LEVELS), F32),
            pltpu.VMEM((1, LEVELS), F32),
            pltpu.VMEM((2, 2, 4, PSLOT), F32),
            pltpu.VMEM((2, 2, 64, HALF), BF16),
            pltpu.VMEM((TILES, 8, 128), F32),
            pltpu.VMEM((2, 2, ROWS, SPAN), BF16),
            pltpu.VMEM((2, SPAN, 2 * WAVES), BF16),
            pltpu.VMEM((SPAN, 2 * WAVES), BF16),
            pltpu.VMEM((2, 2 * WAVES, SPAN), BF16),
            pltpu.VMEM((2, TILES, 2, BLOCKS, 8, 128), F32),
            pltpu.VMEM((2, 128, 128), F32),
            pltpu.VMEM((8 * NB, 128), F32),
            pltpu.VMEM((NB, 8, 128), BF16),
            pltpu.VMEM((NB, 8, 128), BF16),
            pltpu.VMEM((NL, 16, 128), BF16),
            pltpu.VMEM((NL, 16, 128), BF16),
            pltpu.VMEM((NL, 16, 128), BF16),
            pltpu.VMEM((NL, 16, 128), BF16),
            pltpu.VMEM((NB, 8, 128), BF16),
            pltpu.VMEM((NB, 8, 128), BF16),
            pltpu.VMEM((256, HALF), BF16),
            pltpu.VMEM((512, 256), BF16),
            pltpu.VMEM((512, 256), BF16),
            pltpu.VMEM((2, 4, 256, 128), F32),
            pltpu.VMEM((2, 256, HALF), BF16),
            pltpu.SemaphoreType.DMA((8,)),
            pltpu.SemaphoreType.DMA((4,)),
            pltpu.SemaphoreType.DMA((4,)),
        ],
        compiler_params=pltpu.CompilerParams(
            collective_id=0, has_side_effects=True, vmem_limit_bytes=60 * 1024 * 1024
        ),
        cost_estimate=pl.CostEstimate(flops=4_000_000_000, bytes_accessed=1_500_000, transcendentals=0),
    )(
        grid_values, quad_weight, legendre, vertical_modes, eigenvalues.reshape(1, LEVELS),
        pair_latitude, wave_slot.reshape(8, 128), wave_slot,
    )


def solution(mesh):
    in_specs = (
        P("blk", None, "lev", None),
        P("blk"),
        P("blk", None, None, None),
        P(),
        P(),
        P("blk"),
        P(),
    )
    out_specs = P("blk", None, "lev", None)
    return jax.shard_map(shards, mesh=mesh, in_specs=in_specs, out_specs=out_specs, check_vma=False)
```

```python
import jax
import jax.numpy as jnp
from jax import lax
from jax.experimental import pallas as pl
from jax.experimental.pallas import tpu as pltpu
from jax.sharding import PartitionSpec as P

MESH = pl.DeviceIdType.MESH
BF16 = jnp.bfloat16
F32 = jnp.float32

WAVES = 1024
HALF = 512
LEVELS = 64
NB = 32
NL = 16
SPAN = 256
BLOCKS = 22
ROWS = 8 * BLOCKS
TILES = WAVES // 128
LIVE = BLOCKS * SPAN
PSLOT = 6144
IMPLICIT_FACTOR = 4.0
PI = 3.141592653589793


def ring(step, size):
    return min(step, size - step)


BLK_PEERS = sorted(
    [(y, x) for y in range(8) for x in range(4) if (y, x) != (0, 0)],
    key=lambda d: (-ring(d[0], 8) - ring(d[1], 4), d),
)
LEV_PEERS = sorted(
    [(z, c) for z in range(8) for c in range(2) if (z, c) != (0, 0)],
    key=lambda d: (-ring(d[0], 8) - 0.5 * d[1], d),
)


def blk_peer(blk, peer):
    return (blk // 4 + peer[0]) % 8 * 4 + (blk % 4 + peer[1]) % 4


def lev_peer(lev, peer):
    return (lev // 2 + peer[0]) % 8 * 2 + (lev % 2 + peer[1]) % 2


def iota(shape, dim):
    return lax.broadcasted_iota(jnp.int32, shape, dim)


def dot(a, b):
    return jnp.dot(a, b, preferred_element_type=F32)


def dot_nt(a, b):
    return lax.dot_general(a, b, (((1,), (1,)), ((), ())), preferred_element_type=F32)


def dot_tn(a, b):
    return lax.dot_general(a, b, (((0,), (0,)), ((), ())), preferred_element_type=F32)


def split(x):
    high = x.astype(BF16)
    return high, (x - high.astype(F32)).astype(BF16)


def rotation(phase, points, inverse):
    turns = jnp.floor(phase * inverse + 0.5)
    x = (phase - turns * points) * inverse
    z = x * x
    sine = 0.0
    cosine = 0.0
    sin_terms = [PI]
    cos_terms = [1.0]
    for k in range(1, 7):
        sin_terms.append(-sin_terms[-1] * PI * PI / ((2 * k) * (2 * k + 1)))
        cos_terms.append(-cos_terms[-1] * PI * PI / ((2 * k - 1) * (2 * k)))
    sine = jnp.full_like(z, sin_terms[6])
    cosine = jnp.full_like(z, cos_terms[6])
    for k in range(5, -1, -1):
        sine = sine * z + sin_terms[k]
        cosine = cosine * z + cos_terms[k]
    sine = sine * x
    return 1.0 - 2.0 * sine * sine, -2.0 * sine * cosine


def turn(a, b):
    return a[0] * b[0] - a[1] * b[1], a[0] * b[1] + a[1] * b[0]


def stack(parts):
    return jnp.concatenate(parts, axis=0)


def kernel(
    grid_hbm, weight_hbm, legendre_hbm, modes_hbm, rates_hbm, cycle_hbm, slot_hbm, slots_hbm,
    out_ref,
    weight_ref, cycle_ref, slot_smem, slot_ref, modes_ref, rates_ref, grid_ref, raw_ref, wave_ref, x_ref, table_ref, rest_ref, flip_ref, turn_ref, four_ref,
    rows_ref, s1_ref, r1_ref, s2_ref, r2_ref, s3_ref, r3_ref, s4_ref, r4_ref,
    leg_ref, mode1_ref, mode2_ref, damp_ref, solved_ref,
    load_sem, send_sem, recv_sem,
):
    blk = lax.axis_index("blk")
    lev = lax.axis_index("lev")

    barrier = pltpu.get_barrier_semaphore()
    for peer in BLK_PEERS:
        pl.semaphore_signal(barrier, inc=1, device_id=(blk_peer(blk, peer), lev), device_id_type=MESH)
    for peer in LEV_PEERS:
        pl.semaphore_signal(barrier, inc=1, device_id=(blk, lev_peer(lev, peer)), device_id_type=MESH)

    small = [
        (slot_hbm, slot_ref), (cycle_hbm, cycle_ref), (weight_hbm, weight_ref),
        (slots_hbm, slot_smem), (modes_hbm, modes_ref), (rates_hbm, rates_ref),
    ]
    small_copies = [pltpu.make_async_copy(a, b, load_sem.at[2 + k]) for k, (a, b) in enumerate(small)]
    for copy in small_copies:
        copy.start()
    grid_copy = pltpu.make_async_copy(grid_hbm, grid_ref, load_sem.at[0])
    grid_copy.start()
    legendre_copy = pltpu.make_async_copy(
        legendre_hbm.at[pl.ds(2 * lev, 2)], raw_ref, load_sem.at[1]
    )
    legendre_copy.start()
    column = iota((128, WAVES), 1)
    pick = (iota((128, WAVES), 0) == 32 * (column & 3) + (column >> 5)).astype(F32).astype(BF16)
    for copy in small_copies[:3]:
        copy.wait()
    slots = slot_ref[...]
    halves = stack([slots >> 5, slots & 31]).astype(F32).astype(BF16)
    spread = dot(halves, pick)
    column = iota((8, WAVES), 1)
    mine = iota((8, WAVES), 0) == ((column & 31) >> 2)
    spread = jnp.where(mine, 32.0 * spread[:8] + spread[8:], 0.0)
    waves = jnp.sum(spread, axis=0, keepdims=True)
    for tile in range(TILES):
        wave_ref[tile] = jnp.broadcast_to(waves[:, 128 * tile : 128 * (tile + 1)], (8, 128))

    def points_of(i):
        return 20 + 4 * cycle_ref[i]

    def rotations(i, tile):
        points = jnp.full((8, 128), points_of(i), jnp.int32).astype(F32)
        inverse = 1.0 / points
        wave = wave_ref[tile]
        row = iota((8, 128), 0)
        place = row.astype(F32)
        extra = jnp.where(row == 0, 8.0, jnp.where(row == 1, 128.0, 2048.0))
        fine = rotation(place * wave, points, inverse)
        coarse = rotation(16.0 * place * wave, points, inverse)
        block = rotation(256.0 * place * wave, points, inverse)
        jump = rotation(extra * wave, points, inverse)

        def spread_row(pair, k):
            return tuple(jnp.broadcast_to(part[k : k + 1], (8, 128)) for part in pair)

        fine_next = turn(fine, spread_row(jump, 0))
        coarse_next = turn(coarse, spread_row(jump, 1))
        leap = spread_row(jump, 2)
        kept = (2.0 * wave < points).astype(F32)
        block = (block[0] * kept, block[1] * kept)
        block_1 = turn(block, leap)
        block_2 = turn(block_1, leap)

        high = [[], []]
        low = [[], []]
        for a in range(16):
            lead = spread_row(coarse if a < 8 else coarse_next, a % 8)
            first = turn(lead, fine)
            second = turn(lead, fine_next)
            for part in range(2):
                h, l = split(stack([first[part], second[part]]))
                high[part].append(h)
                low[part].append(l)
        table = jnp.concatenate([stack(high[0]), stack(high[1])], axis=1)
        rest = jnp.concatenate([stack(low[0]), stack(low[1])], axis=1)
        table_ref[i, :, pl.ds(pl.multiple_of(256 * tile, 256), 256)] = table
        turns = [spread_row((block, block_1, block_2)[u // 8], u % 8) for u in range(BLOCKS)]
        for u in range(BLOCKS):
            turn_ref[i, tile, 0, u], turn_ref[i, tile, 1, u] = turns[u]
        return table, rest, turns

    def transform(i, tile, table, rest, turns):
        x_high = x_ref[i, 0]
        sums = dot(
            jnp.concatenate([x_high, x_ref[i, 1], x_high], axis=1),
            jnp.concatenate([table, table, rest], axis=0),
        )
        real = jnp.zeros((8, 128), F32)
        imag = jnp.zeros((8, 128), F32)
        for u in range(BLOCKS):
            c, s = turns[u]
            p, q = sums[8 * u : 8 * u + 8, :128], sums[8 * u : 8 * u + 8, 128:]
            real = real + (c * p - s * q)
            imag = imag + (c * q + s * p)
        start = pl.multiple_of(16 * tile, 16)
        four_ref[i, pl.ds(start, 8), :] = real
        four_ref[i, pl.ds(start + 8, 8), :] = imag

    def early_step(tile, carry):
        _, rest, _ = rotations(0, tile)
        rest_ref[:, pl.ds(pl.multiple_of(256 * tile, 256), 256)] = rest
        return carry

    lax.fori_loop(0, 8, early_step, 0, unroll=4)

    grid_copy.wait()

    def fold_step(step, carry):
        i = step // (BLOCKS // 2)
        k = step % (BLOCKS // 2)
        points = points_of(i)
        scale = jnp.full((4, SPAN), weight_ref[i], F32) / jnp.full((4, SPAN), points, jnp.int32).astype(F32)
        rows = []
        for half in range(2):
            start = pl.multiple_of(512 * k + 256 * half, 256)
            live = iota((4, SPAN), 1) + start < points
            north = grid_ref[i, 0, :, pl.ds(start, SPAN)]
            south = grid_ref[i, 1, :, pl.ds(start, SPAN)]
            rows.append(jnp.where(live, (north + south) * scale, 0.0))
            rows.append(jnp.where(live, (north - south) * scale, 0.0))
        high, low = split(stack(rows))
        x_ref[i, 0, pl.ds(pl.multiple_of(16 * k, 16), 16), :] = high
        x_ref[i, 1, pl.ds(pl.multiple_of(16 * k, 16), 16), :] = low
        return carry

    lax.fori_loop(0, BLOCKS, fold_step, 0, unroll=2)

    def early_transform(tile, carry):
        lanes = pl.ds(pl.multiple_of(256 * tile, 256), 256)
        turns = [(turn_ref[0, tile, 0, u], turn_ref[0, tile, 1, u]) for u in range(BLOCKS)]
        transform(0, tile, table_ref[0, :, lanes], rest_ref[:, lanes], turns)
        return carry

    def analyse_step(step, carry):
        transform(step // TILES, step % TILES, *rotations(step // TILES, step % TILES))
        return carry

    lax.fori_loop(0, 8, early_transform, 0, unroll=4)
    lax.fori_loop(8, 2 * TILES, analyse_step, 0, unroll=4)

    for i in range(2):
        flipped = four_ref[i].T
        for a in range(4):
            rows_ref[pl.ds(2 * a + i, NB, stride=8), :] = flipped[NB * a : NB * (a + 1)]
    s1_ref[...] = rows_ref[...].astype(BF16).reshape(NB, 8, 128)
    r1_ref[blk] = s1_ref[blk]
    pl.semaphore_wait(barrier, NB + NL - 2)

    def send_blk(source, target, sem):
        for peer in BLK_PEERS:
            other = blk_peer(blk, peer)
            pltpu.make_async_remote_copy(
                src_ref=source.at[other],
                dst_ref=target.at[blk],
                send_sem=send_sem.at[sem],
                recv_sem=recv_sem.at[sem],
                device_id=(other, lev),
                device_id_type=MESH,
            ).start()
        rows = pl.ds(0, NB - 1)
        return pltpu.make_async_remote_copy(
            src_ref=source.at[rows], dst_ref=target.at[rows],
            send_sem=send_sem.at[sem], recv_sem=recv_sem.at[sem],
            device_id=(blk_peer(blk, BLK_PEERS[0]), lev), device_id_type=MESH,
        )

    def send_lev(source, target, sem):
        for peer in LEV_PEERS:
            other = lev_peer(lev, peer)
            pltpu.make_async_remote_copy(
                src_ref=source.at[other],
                dst_ref=target.at[lev],
                send_sem=send_sem.at[sem],
                recv_sem=recv_sem.at[sem],
                device_id=(blk, other),
                device_id_type=MESH,
            ).start()
        rows = pl.ds(0, NL - 1)
        return pltpu.make_async_remote_copy(
            src_ref=source.at[rows], dst_ref=target.at[rows],
            send_sem=send_sem.at[sem], recv_sem=recv_sem.at[sem],
            device_id=(blk, lev_peer(lev, LEV_PEERS[0])), device_id_type=MESH,
        )

    sent_1 = send_blk(s1_ref, r1_ref, 0)

    legendre_copy.wait()
    for copy in small_copies[3:]:
        copy.wait()
    wave_0 = slot_smem[32 * blk + 2 * lev]
    wave_1 = slot_smem[32 * blk + 2 * lev + 1]
    row = iota((256, 256), 0)
    source = ((row >> 6) & 1) * 128 + (row >> 7) * 64 + 2 * (row & 31) + ((row >> 5) & 1)
    reorder = (iota((256, 256), 1) == source).astype(F32).astype(BF16)
    ordered = dot(reorder, raw_ref[...].reshape(256, HALF))
    row = iota((256, HALF), 0)
    degree = jnp.where(((row >> 6) & 1) == 0, wave_0, wave_1) + (row >> 7) + 2 * iota((256, HALF), 1)
    leg_ref[...] = jnp.where(degree <= WAVES - 1, ordered, 0.0).astype(BF16)

    def spread_rows(shape, row_dim):
        row = iota(shape, row_dim)
        return iota(shape, 1 - row_dim) == 4 * (row >> 4) + (row & 3)

    tall = spread_rows((256, LEVELS), 0).astype(F32).astype(BF16)
    wide = spread_rows((LEVELS, 256), 1).astype(F32).astype(BF16)
    same = ((iota((256, 256), 0) >> 2) & 3) == ((iota((256, 256), 1) >> 2) & 3)
    for part, modes in enumerate(split(modes_ref[...])):
        full = dot(tall, dot(modes, wide).astype(BF16))
        mode2_ref[256 * part : 256 * (part + 1), :] = jnp.where(same, full, 0.0).astype(BF16)
        full = dot(tall, dot_tn(modes, wide).astype(BF16))
        mode1_ref[256 * part : 256 * (part + 1), :] = jnp.where(same, full, 0.0).astype(BF16)

    rate = jnp.sum(
        jnp.where(spread_rows((256, LEVELS), 0), jnp.broadcast_to(rates_ref[...], (256, LEVELS)), 0.0),
        axis=1, keepdims=True,
    )
    rate = jnp.broadcast_to(rate, (256, 128))

    def damp_step(step, carry):
        e = step // 4
        chunk = step % 4
        wave = jnp.where(e == 0, wave_0, wave_1)
        degree = wave + ((iota((256, 128), 0) >> 2) & 1) + 2 * (iota((256, 128), 1) + 128 * chunk)
        degree = degree.astype(F32)
        term = degree * (degree + 1.0) * (IMPLICIT_FACTOR / (WAVES * (WAVES - 1)))
        stiffness = term * rate
        damp_ref[e, chunk] = stiffness / (1.0 + stiffness)
        return carry

    lax.fori_loop(0, 8, damp_step, 0)

    def flip_step(step, carry):
        i = step // TILES
        tile = step % TILES
        lanes = pl.ds(pl.multiple_of(256 * tile, 256), 256)
        flip_ref[i, lanes, :] = table_ref[i, :, lanes].T
        return carry

    lax.fori_loop(0, 2 * TILES, flip_step, 0)

    sent_1.wait_recv()

    rows_ref[...] = r1_ref[...].reshape(8 * NB, 128).astype(F32)
    for a in range(2):
        block = stack([rows_ref[pl.ds(4 * a + j, NB, stride=8), :] for j in range(4)]).T.astype(BF16)
        for t in range(8):
            s2_ref[2 * t + a] = block[16 * t : 16 * (t + 1)]
    r2_ref[lev] = s2_ref[lev]
    sent_2 = send_lev(s2_ref, r2_ref, 1)
    sent_2.wait_recv()

    data = r2_ref[...].reshape(256, 128)
    parity = (iota((256, 128), 0) >> 2) & 1
    side = iota((256, 128), 1) >> 6

    def chosen(q, e):
        return ((parity == q) & (side == e)).astype(F32).astype(BF16)

    jobs = [(e, step) for step in range(2) for e in range(2)]
    lefts = [jnp.concatenate([data * chosen(q, e) for q in range(2)], axis=1) for e in range(2)]
    spectral = [dot(lefts[e], leg_ref[:, 256 * step : 256 * (step + 1)]) for e, step in jobs]
    modal = [dot(mode1_ref[...], part.astype(BF16)) for part in spectral]
    modal = [part[:256] + part[256:] for part in modal]
    for k, (e, step) in enumerate(jobs):
        damping = jnp.concatenate([damp_ref[e, 2 * step], damp_ref[e, 2 * step + 1]], axis=1)
        modal[k] = (modal[k] * damping).astype(BF16)
    for k, (e, step) in enumerate(jobs):
        change = dot(mode2_ref[...], modal[k])
        solved = spectral[k] - (change[:256] + change[256:])
        solved_ref[e, :, 256 * step : 256 * (step + 1)] = solved.astype(BF16)

    picked = []
    for e in range(2):
        back = dot_nt(solved_ref[e], leg_ref[...])
        picked.append(jnp.where(parity == 0, back[:, :128], back[:, 128:]))
    s3_ref[...] = jnp.where(side == 0, picked[0], picked[1]).astype(BF16).reshape(NL, 16, 128)
    r3_ref[lev] = s3_ref[lev]
    sent_3 = send_lev(s3_ref, r3_ref, 2)
    sent_3.wait_recv()

    for a in range(2):
        block = stack([r3_ref[2 * t + a] for t in range(8)]).astype(F32).T
        for j in range(4):
            rows_ref[pl.ds(4 * a + j, NB, stride=8), :] = block[NB * j : NB * (j + 1)]
    s4_ref[...] = rows_ref[...].astype(BF16).reshape(NB, 8, 128)
    r4_ref[blk] = s4_ref[blk]
    sent_4 = send_blk(s4_ref, r4_ref, 3)
    out_ref[:, :, :, pl.ds(LIVE, PSLOT - LIVE)] = jnp.zeros((2, 2, 4, PSLOT - LIVE), F32)
    sent_4.wait_recv()

    rows_ref[...] = r4_ref[...].reshape(8 * NB, 128).astype(F32)
    for i in range(2):
        four_ref[i] = stack([rows_ref[pl.ds(2 * a + i, NB, stride=8), :] for a in range(4)]).T

    for i in range(2):
        points = points_of(i)
        value = 0.0
        for group in range(2):
            left = []
            for tile in range(4 * group, 4 * group + 4):
                double = jnp.where(wave_ref[tile] == 0.0, 1.0, 2.0)
                real = four_ref[i, 16 * tile : 16 * tile + 8, :] * double
                imag = four_ref[i, 16 * tile + 8 : 16 * tile + 16, :] * double
                reals, imags = [], []
                for u in range(BLOCKS):
                    c = turn_ref[i, tile, 0, u]
                    s = turn_ref[i, tile, 1, u]
                    reals.append(real * c + imag * s)
                    imags.append(imag * c - real * s)
                left += [stack(reals).astype(BF16), stack(imags).astype(BF16)]
            right = flip_ref[i, 1024 * group : 1024 * (group + 1), :]
            value = value + dot(jnp.concatenate(left, axis=1), right)
        for u in range(BLOCKS):
            even = value[8 * u : 8 * u + 4]
            odd = value[8 * u + 4 : 8 * u + 8]
            live = iota((4, SPAN), 1) + SPAN * u < points
            out_ref[i, 0, :, SPAN * u : SPAN * (u + 1)] = jnp.where(live, even + odd, 0.0)
            out_ref[i, 1, :, SPAN * u : SPAN * (u + 1)] = jnp.where(live, even - odd, 0.0)

    for sent in (sent_1, sent_2, sent_3, sent_4):
        sent.wait_send()


def shards(grid_values, quad_weight, legendre, vertical_modes, eigenvalues, pair_latitude, wave_slot):
    vmem = pl.BlockSpec(memory_space=pltpu.VMEM)
    hbm = pl.BlockSpec(memory_space=pl.ANY)
    return pl.pallas_call(
        kernel,
        out_shape=pltpu.VMEM(grid_values.shape, F32),
        in_specs=[hbm] * 8,
        out_specs=vmem,
        scratch_shapes=[
            pltpu.SMEM((2,), F32),
            pltpu.SMEM((2,), jnp.int32),
            pltpu.SMEM((WAVES,), jnp.int32),
            pltpu.VMEM((8, 128), jnp.int32),
            pltpu.VMEM((LEVELS, LEVELS), F32),
            pltpu.VMEM((1, LEVELS), F32),
            pltpu.VMEM((2, 2, 4, PSLOT), F32),
            pltpu.VMEM((2, 2, 64, HALF), BF16),
            pltpu.VMEM((TILES, 8, 128), F32),
            pltpu.VMEM((2, 2, ROWS, SPAN), BF16),
            pltpu.VMEM((2, SPAN, 2 * WAVES), BF16),
            pltpu.VMEM((SPAN, 2 * WAVES), BF16),
            pltpu.VMEM((2, 2 * WAVES, SPAN), BF16),
            pltpu.VMEM((2, TILES, 2, BLOCKS, 8, 128), F32),
            pltpu.VMEM((2, 128, 128), F32),
            pltpu.VMEM((8 * NB, 128), F32),
            pltpu.VMEM((NB, 8, 128), BF16),
            pltpu.VMEM((NB, 8, 128), BF16),
            pltpu.VMEM((NL, 16, 128), BF16),
            pltpu.VMEM((NL, 16, 128), BF16),
            pltpu.VMEM((NL, 16, 128), BF16),
            pltpu.VMEM((NL, 16, 128), BF16),
            pltpu.VMEM((NB, 8, 128), BF16),
            pltpu.VMEM((NB, 8, 128), BF16),
            pltpu.VMEM((256, HALF), BF16),
            pltpu.VMEM((512, 256), BF16),
            pltpu.VMEM((512, 256), BF16),
            pltpu.VMEM((2, 4, 256, 128), F32),
            pltpu.VMEM((2, 256, HALF), BF16),
            pltpu.SemaphoreType.DMA((8,)),
            pltpu.SemaphoreType.DMA((4,)),
            pltpu.SemaphoreType.DMA((4,)),
        ],
        compiler_params=pltpu.CompilerParams(
            collective_id=0, has_side_effects=True, vmem_limit_bytes=60 * 1024 * 1024
        ),
        cost_estimate=pl.CostEstimate(flops=4_000_000_000, bytes_accessed=1_500_000, transcendentals=0),
    )(
        grid_values, quad_weight, legendre, vertical_modes, eigenvalues.reshape(1, LEVELS),
        pair_latitude, wave_slot.reshape(8, 128), wave_slot,
    )


def solution(mesh):
    in_specs = (
        P("blk", None, "lev", None),
        P("blk"),
        P("blk", None, None, None),
        P(),
        P(),
        P("blk"),
        P(),
    )
    out_specs = P("blk", None, "lev", None)
    return jax.shard_map(shards, mesh=mesh, in_specs=in_specs, out_specs=out_specs, check_vma=False)
```
